512 devices in a mesh: loop: 16 (over x, z_lo), bulk: 32 (over z_hi, y, core).
Axes of the slice: x: 4, y: 8, z: 8 (z_hi: 2, z_lo: 4; z = z_hi * 4 + z_lo), core: 2. Of those that a mesh axis runs over, the one named last changes fastest.
Arguments:
- series: float32 [16896, 3072], P('loop', 'bulk'), may hold values from -64 to 64
Outputs:
- correlation: float32 [16, 1056, 16896], P(None, 'bulk', 'loop')
The draws below stay inside these ranges and needn't reach their ends.
All inputs are finite; a program needn't handle non-finite values.
Results may differ from the reference program's by a relative error of at most 0.0011.
Values may be sent and summed in bfloat16 or wider, within the bound.
No kernel may reach another device: no remote copies, remote signals or barrier semaphores. Data moves between devices by JAX's collectives and lax.ppermute only.
A program may use at most 64 MiB of HBM per device.

```python
import jax
import jax.numpy as jnp
from jax import lax

ROWS_DEV = 1056
TIME = 3072
GRAY = 16896
N_LOOP = 16


def draw_series(key, part):
    keys = jax.random.split(key, 3)
    position = (jnp.arange(TIME, dtype=jnp.float32) + 0.5) / TIME
    ramp = (0.5 + position)[None, :]
    drift = jax.random.truncated_normal(keys[1], -3.0, 3.0, (GRAY, 1), jnp.float32)
    scale_row = jnp.exp(jax.random.uniform(keys[0], (GRAY, 1), jnp.float32, 0.0, jnp.log(10.0)))
    noise = jax.random.truncated_normal(keys[2], -4.0, 4.0, (GRAY, TIME), jnp.float32)
    values = scale_row * (drift * ramp + jnp.sqrt(ramp) * noise)
    return jnp.clip(values, -64.0, 64.0)


def setup_inputs(seed: int = 0) -> dict:
    key_of = jax.random.split(jax.random.key(seed), 2)
    series = draw_series(jax.random.fold_in(key_of[1], 71), 0)
    return dict(series=series)


epsilon = 1e-06

def reference(series):
    average = lax.optimization_barrier(jnp.sum(series, axis=1, keepdims=True)) / TIME
    centered = series - average
    variance = lax.optimization_barrier(jnp.sum(centered * centered, axis=1, keepdims=True)) / TIME
    zscore = (centered * lax.rsqrt(variance + epsilon)).astype(jnp.bfloat16)
    gray_blocks = zscore.reshape(N_LOOP, ROWS_DEV, TIME)

    def block_product(gray_block):
        product = lax.dot_general(gray_block, zscore, (((1,), (1,)), ((), ())), preferred_element_type=jnp.float32)
        return product / TIME
    return lax.map(block_product, gray_blocks)
```

```python
import jax
import jax.numpy as jnp
from jax import lax
from jax.sharding import PartitionSpec as P

TIME = 3072

epsilon = 1e-06


def standardize(rows):
    average = jnp.sum(rows, axis=1, keepdims=True) / TIME
    centered = rows - average
    variance = jnp.sum(centered * centered, axis=1, keepdims=True) / TIME
    return (centered * lax.rsqrt(variance + epsilon)).astype(jnp.bfloat16)


def on_device(series):
    n_bulk = lax.axis_size("bulk")
    rows, steps = series.shape
    share = rows // n_bulk
    pieces = lax.all_to_all(series.reshape(n_bulk, share, steps), "bulk", 0, 0, tiled=True)
    own = standardize(pieces.transpose(1, 0, 2).reshape(share, n_bulk * steps))
    block = lax.all_gather(own, "bulk", axis=0, tiled=True)
    others = lax.all_gather(own, "loop", axis=0, tiled=True)
    product = lax.dot_general(
        others, block, (((1,), (1,)), ((), ())), preferred_element_type=jnp.float32
    )
    return (product / TIME).reshape(lax.axis_size("loop"), share, rows)


def solution(mesh):
    placed = (P("loop", "bulk"),)
    return jax.shard_map(
        on_device, mesh=mesh, in_specs=placed, out_specs=P(None, "bulk", "loop"), check_vma=False
    )
```

```python
import jax
import jax.numpy as jnp
from jax import lax
from jax.sharding import Mesh, PartitionSpec as P

TIME = 3072
AXES = ("x", "zl", "zh", "y", "core")
SIZES = (4, 4, 2, 8, 2)

epsilon = 1e-06


def standardize(rows):
    average = jnp.sum(rows, axis=1, keepdims=True) / TIME
    centered = rows - average
    variance = jnp.sum(centered * centered, axis=1, keepdims=True) / TIME
    return (centered * lax.rsqrt(variance + epsilon)).astype(jnp.bfloat16)


def shift(array, axis, by):
    size = lax.axis_size(axis)
    return lax.ppermute(array, axis, [(i, (i + by) % size) for i in range(size)])


def gather_x(part):
    after = shift(part, "x", 1)
    before = shift(part, "x", -1)
    half = part.shape[0] // 2
    far = jnp.concatenate([shift(after[:half], "x", 1), shift(before[half:], "x", -1)])
    here = lax.axis_index("x")
    whole = jnp.zeros((4,) + part.shape, part.dtype)
    for piece, offset in ((part, 0), (after, -1), (far, 2), (before, 1)):
        whole = lax.dynamic_update_slice_in_dim(whole, piece[None], (here + offset) % 4, 0)
    return whole.reshape((4 * part.shape[0],) + part.shape[1:])


def on_device(series):
    rows, steps = series.shape
    share = rows // 32
    bulk = ("zh", "y", "core")
    pieces = lax.all_to_all(series.reshape(32, share, steps), bulk, 0, 0, tiled=True)
    own = standardize(pieces.transpose(1, 0, 2).reshape(share, TIME))
    pair = lax.all_gather(own, "zh")
    block = lax.all_gather(pair, ("y", "core"))
    block = block.transpose(1, 0, 2, 3).reshape(rows, TIME)
    others = gather_x(lax.all_gather(own, "zl"))
    product = lax.dot_general(
        others, block, (((2,), (1,)), ((), ())), preferred_element_type=jnp.float32
    )
    return product / TIME


def solution(mesh):
    split = Mesh(mesh.devices.reshape(SIZES), AXES)
    return jax.shard_map(
        on_device,
        mesh=split,
        in_specs=(P(("x", "zl"), ("zh", "y", "core")),),
        out_specs=P(None, ("zh", "y", "core"), ("x", "zl")),
        check_vma=False,
    )
```

```python
import jax
import jax.numpy as jnp
from jax import lax
from jax.experimental import pallas as pl
from jax.experimental.pallas import tpu as pltpu
from jax.sharding import Mesh, PartitionSpec as P

TIME = 3072
AXES = ("x", "zl", "zh", "y", "core")
SIZES = (4, 4, 2, 8, 2)
BULK = ("zh", "y", "core")
SHARE = 33
WINDOW = 40
ROWS = 1056
GROUP = 8 * SHARE

epsilon = 1e-06


def standardize(rows):
    average = jnp.sum(rows, axis=1, keepdims=True) / TIME
    centered = rows - average
    variance = jnp.sum(centered * centered, axis=1, keepdims=True) / TIME
    return (centered * lax.rsqrt(variance + epsilon)).astype(jnp.bfloat16)


def shift(array, axis, by):
    size = lax.axis_size(axis)
    return lax.ppermute(array, axis, [(i, (i + by) % size) for i in range(size)])


def gather_x(part):
    after = shift(part, "x", 1)
    before = shift(part, "x", -1)
    far = [shift(after[:, :2], "x", 1), shift(before[:, 2:], "x", -1)]
    return jnp.concatenate([part, before, *far, after], axis=1)


def product_kernel(place, others, windows, out, held, block, arrived):
    copies = []
    for group in range(4):
        half, parity = divmod(group, 2)
        copy = pltpu.make_async_copy(
            windows.at[pl.ds(8 * parity, 8), half], held.at[group], arrived.at[group]
        )
        copy.start()
        copies.append(copy)
    edges = [0, 256, 512, 768, ROWS]
    for group in range(4):
        copies[group].wait()
        for i in range(8):
            start = GROUP * group + 32 * i
            size = 32 if i < 7 else 40
            block[start : start + size, :] = held[group, i, :size, :]
        low, high = edges[group], edges[group + 1]
        product = lax.dot_general(
            others[...],
            block[low:high, :],
            (((1,), (1,)), ((), ())),
            preferred_element_type=jnp.float32,
        ) * (1.0 / TIME)
        product = product.reshape(SHARE, 16, high - low)
        for x in range(4):

            @pl.when(place[0] == x)
            def _():
                for k in range(4):
                    to = 4 * ((x + k) % 4)
                    out[:, to : to + 4, low:high] = product[:, 4 * k : 4 * k + 4, :]


def multiply(others, windows):
    place = lax.axis_index("x").astype(jnp.int32).reshape(1)
    return pl.pallas_call(
        product_kernel,
        out_shape=jax.ShapeDtypeStruct((SHARE, 16, ROWS), jnp.float32),
        in_specs=[
            pl.BlockSpec(memory_space=pltpu.SMEM),
            pl.BlockSpec(memory_space=pltpu.VMEM),
            pl.BlockSpec(memory_space=pl.ANY),
        ],
        out_specs=pl.BlockSpec(memory_space=pltpu.VMEM),
        scratch_shapes=[
            pltpu.VMEM((4, 8, WINDOW, TIME), jnp.bfloat16),
            pltpu.VMEM((ROWS, TIME), jnp.bfloat16),
            pltpu.SemaphoreType.DMA((4,)),
        ],
        compiler_params=pltpu.CompilerParams(vmem_limit_bytes=48 * 1024 * 1024),
        cost_estimate=pl.CostEstimate(
            flops=2 * 528 * ROWS * TIME, bytes_accessed=14_000_000, transcendentals=0
        ),
    )(place, others, windows)


def on_device(series):
    groups = series.reshape(4, GROUP, -1)
    windows = jnp.stack([groups[:, 32 * i : 32 * i + WINDOW] for i in range(8)], axis=1)
    windows = windows.reshape(32, WINDOW, -1)
    pieces = lax.all_to_all(windows, BULK, 0, 0, tiled=True)
    window = standardize(pieces.transpose(1, 0, 2).reshape(WINDOW, TIME))
    own = lax.dynamic_slice_in_dim(window, lax.rem(lax.axis_index(BULK), 8), SHARE, 0)
    pair = lax.all_gather(window, "zh")
    gathered = lax.all_gather(pair, ("y", "core"))
    others = gather_x(lax.all_gather(own, "zl").transpose(1, 0, 2))
    product = multiply(others.reshape(SHARE * 16, TIME), gathered)
    return product.transpose(1, 0, 2)


def solution(mesh):
    split = Mesh(mesh.devices.reshape(SIZES), AXES)
    return jax.shard_map(
        on_device,
        mesh=split,
        in_specs=(P(("x", "zl"), BULK),),
        out_specs=P(None, BULK, ("x", "zl")),
        check_vma=False,
    )
```

```python
import jax
import jax.numpy as jnp
from jax import lax
from jax.experimental import pallas as pl
from jax.experimental.pallas import tpu as pltpu
from jax.sharding import Mesh, PartitionSpec as P

TIME = 3072
HALF = TIME // 2
AXES = ("x", "zl", "zh", "y", "core")
SIZES = (4, 4, 2, 8, 2)
BULK = ("zh", "y", "core")
SHARE = 33
WINDOW = 40
ROWS = 1056
GROUP = 8 * SHARE

epsilon = 1e-06


def shift(array, axis, by):
    size = lax.axis_size(axis)
    return lax.ppermute(array, axis, [(i, (i + by) % size) for i in range(size)])


def standardize(half):
    mean = jnp.sum(half, axis=1) / HALF
    from_mean = half - mean[:, None]
    deviation = jnp.sum(from_mean * from_mean, axis=1)
    both = lax.all_gather(jnp.stack([mean, deviation]), "zh")
    average = (both[0, 0] + both[1, 0]) * 0.5
    between = both[0, 0] - both[1, 0]
    squares = both[0, 1] + both[1, 1] + (HALF * 0.5) * (between * between)
    scale = lax.rsqrt(squares / TIME + epsilon)
    return ((half - average[:, None]) * scale[:, None]).astype(jnp.bfloat16)


def gather_x(part):
    after = shift(part, "x", 1)
    before = shift(part, "x", -1)
    far = [shift(after[:, :2], "x", 1), shift(before[:, 2:], "x", -1)]
    return jnp.concatenate([part, before, *far, after], axis=1)


def product_kernel(place, others, near, far, out, held_near, held_far, block, arrived):
    copies = []
    for h in range(2):
        for n, (source, held) in enumerate(((near, held_near), (far, held_far))):
            yc = pl.ds(8 * h, 8)
            copy = pltpu.make_async_copy(source.at[yc], held.at[yc], arrived.at[2 * h + n])
            copy.start()
            copies.append(copy)
    for h in range(2):
        copies[2 * h].wait()
        copies[2 * h + 1].wait()
        for w in range(2):
            for i in range(8):
                start = GROUP * (2 * w + h) + 32 * i
                size = 32 if i < 7 else 40
                rows = slice(WINDOW * w, WINDOW * w + size)
                block[start : start + size, :HALF] = held_near[8 * h + i, rows, :]
                block[start : start + size, HALF:] = held_far[8 * h + i, rows, :]
    edges = [0, 256, 512, 768, ROWS]
    for low, high in zip(edges[:-1], edges[1:]):
        product = lax.dot_general(
            others[...],
            block[low:high, :],
            (((1,), (1,)), ((), ())),
            preferred_element_type=jnp.float32,
        ) * (1.0 / TIME)
        product = product.reshape(SHARE, 16, high - low)
        for x in range(4):

            @pl.when(place[0] == x)
            def _():
                for k in range(4):
                    to = 4 * ((x + k) % 4)
                    out[:, to : to + 4, low:high] = product[:, 4 * k : 4 * k + 4, :]


def multiply(others, near, far):
    place = lax.axis_index("x").astype(jnp.int32).reshape(1)
    return pl.pallas_call(
        product_kernel,
        out_shape=jax.ShapeDtypeStruct((SHARE, 16, ROWS), jnp.float32),
        in_specs=[
            pl.BlockSpec(memory_space=pltpu.SMEM),
            pl.BlockSpec(memory_space=pltpu.VMEM),
            pl.BlockSpec(memory_space=pl.ANY),
            pl.BlockSpec(memory_space=pl.ANY),
        ],
        out_specs=pl.BlockSpec(memory_space=pltpu.VMEM),
        scratch_shapes=[
            pltpu.VMEM((16, 2 * WINDOW, HALF), jnp.bfloat16),
            pltpu.VMEM((16, 2 * WINDOW, HALF), jnp.bfloat16),
            pltpu.VMEM((ROWS, TIME), jnp.bfloat16),
            pltpu.SemaphoreType.DMA((4,)),
        ],
        compiler_params=pltpu.CompilerParams(vmem_limit_bytes=48 * 1024 * 1024),
        cost_estimate=pl.CostEstimate(
            flops=2 * 528 * ROWS * TIME, bytes_accessed=14_000_000, transcendentals=0
        ),
    )(place, others, near, far)


def on_device(series):
    steps = series.shape[1]
    groups = series.reshape(2, 2, GROUP, steps)
    windows = jnp.stack([groups[:, :, 32 * i : 32 * i + WINDOW] for i in range(8)], axis=2)
    windows = windows.transpose(1, 2, 0, 3, 4).reshape(16, 2 * WINDOW, steps)
    pieces = lax.all_to_all(windows, ("y", "core"), 0, 0, tiled=True)
    zscore = standardize(pieces.transpose(1, 0, 2).reshape(2 * WINDOW, HALF))
    near = lax.all_gather(zscore, ("y", "core"))

    zh, zl = lax.axis_index("zh"), lax.axis_index("zl")
    column = [
        lax.all_gather(zscore[WINDOW * w : WINDOW * w + WINDOW], ("zh", "zl")) for w in range(2)
    ]
    partner = jnp.concatenate(
        [lax.dynamic_index_in_dim(c, (1 - zh) * 4 + zl, 0, False) for c in column]
    )
    far = lax.all_gather(partner, ("y", "core"))

    mine = jnp.where(zh == 0, column[0], column[1]).reshape(2, 4, WINDOW, HALF)
    mine = lax.dynamic_slice_in_dim(mine, lax.rem(lax.axis_index(BULK), 8), SHARE, 2)
    mine = jnp.where(zh == 0, mine, mine[::-1])
    mine = mine.transpose(2, 1, 0, 3).reshape(SHARE, 4, TIME)
    others = gather_x(mine)
    product = multiply(others.reshape(SHARE * 16, TIME), near, far)
    return product.transpose(1, 0, 2)


def solution(mesh):
    split = Mesh(mesh.devices.reshape(SIZES), AXES)
    return jax.shard_map(
        on_device,
        mesh=split,
        in_specs=(P(("x", "zl"), BULK),),
        out_specs=P(None, BULK, ("x", "zl")),
        check_vma=False,
    )
```

```python
import jax
import jax.numpy as jnp
from jax import lax
from jax.experimental import pallas as pl
from jax.experimental.pallas import tpu as pltpu
from jax.sharding import Mesh, PartitionSpec as P

TIME = 3072
HALF = TIME // 2
AXES = ("x", "zl", "zh", "y", "core")
SIZES = (4, 4, 2, 8, 2)
BULK = ("zh", "y", "core")
SHARE = 33
WINDOW = 40
ROWS = 1056
GROUP = 8 * SHARE

epsilon = 1e-06


def shift(array, axis, by):
    size = lax.axis_size(axis)
    return lax.ppermute(array, axis, [(i, (i + by) % size) for i in range(size)])


def pack(windows):
    n = windows.shape[0]
    tail = windows[:, 64:].reshape(n, 16, 3, 32).transpose(0, 2, 1, 3).reshape(n, 48, 32)
    tail = jnp.pad(tail, ((0, 0), (0, 16), (0, 0)))
    return jnp.concatenate([windows[:, :64], tail], axis=2)


def unpack(pieces):
    n = pieces.shape[0]
    tail = pieces[:, :48, 96:].reshape(n, 3, 16, 32).transpose(0, 2, 1, 3).reshape(n, 16, 96)
    return jnp.concatenate([pieces[:, :, :96], tail], axis=1)


def standardize(half):
    mean = jnp.sum(half, axis=1) / HALF
    from_mean = half - mean[:, None]
    deviation = jnp.sum(from_mean * from_mean, axis=1)
    both = lax.all_gather(jnp.stack([mean, deviation]), "zh")
    average = (both[0, 0] + both[1, 0]) * 0.5
    between = both[0, 0] - both[1, 0]
    squares = both[0, 1] + both[1, 1] + (HALF * 0.5) * (between * between)
    scale = lax.rsqrt(squares / TIME + epsilon)
    return ((half - average[:, None]) * scale[:, None]).astype(jnp.bfloat16)


def gather_x(part):
    after = shift(part, "x", 1)
    before = shift(part, "x", -1)
    cut = HALF // 2
    far = [shift(after[:, :cut], "x", 1), shift(before[:, cut:], "x", -1)]
    return jnp.concatenate([part, before, jnp.concatenate(far, axis=1), after], axis=0)


def product_kernel(place, first, second, windows, out, held, block, turned, arrived):
    copies = []
    for h in range(2):
        yc = pl.ds(8 * h, 8)
        copy = pltpu.make_async_copy(windows.at[yc], held.at[yc], arrived.at[h])
        copy.start()
        copies.append(copy)

    def place_rows(h):
        copies[h].wait()
        for w in range(2):
            for i in range(8):
                start = GROUP * (2 * w + h) + 32 * i
                size = 32 if i < 7 else 40
                rows = slice(WINDOW * w, WINDOW * w + size)
                for t in range(2):
                    steps = slice(HALF * t, HALF * t + HALF)
                    block[start : start + size, steps] = held[8 * h + i, t, rows, :]

    def multiply_rows(low, high):
        product = 0.0
        for t, part in enumerate((first, second)):
            product += lax.dot_general(
                part[...],
                block[low:high, HALF * t : HALF * t + HALF],
                (((1,), (1,)), ((), ())),
                preferred_element_type=jnp.float32,
            )
        product = product * (1.0 / TIME)
        for k in range(4):
            turned[k, :, : high - low] = product[132 * k : 132 * k + 132, :]
        for x in range(4):
            rows = turned[lax.rem(x - place[0] + 4, 4), :, : high - low]
            out[:, 4 * x : 4 * x + 4, low:high] = rows.reshape(SHARE, 4, high - low)

    place_rows(0)
    multiply_rows(0, 256)
    place_rows(1)
    multiply_rows(256, 512)
    multiply_rows(512, 768)
    multiply_rows(768, ROWS)


def multiply(first, second, windows):
    place = lax.axis_index("x").astype(jnp.int32).reshape(1)
    return pl.pallas_call(
        product_kernel,
        out_shape=jax.ShapeDtypeStruct((SHARE, 16, ROWS), jnp.float32),
        in_specs=[
            pl.BlockSpec(memory_space=pltpu.SMEM),
            pl.BlockSpec(memory_space=pltpu.VMEM),
            pl.BlockSpec(memory_space=pltpu.VMEM),
            pl.BlockSpec(memory_space=pltpu.HBM),
        ],
        out_specs=pl.BlockSpec(memory_space=pltpu.VMEM),
        scratch_shapes=[
            pltpu.VMEM((16, 2, 2 * WINDOW, HALF), jnp.bfloat16),
            pltpu.VMEM((ROWS, TIME), jnp.bfloat16),
            pltpu.VMEM((4, 4 * SHARE, 384), jnp.float32),
            pltpu.SemaphoreType.DMA((2,)),
        ],
        compiler_params=pltpu.CompilerParams(vmem_limit_bytes=48 * 1024 * 1024),
        cost_estimate=pl.CostEstimate(
            flops=2 * 528 * ROWS * TIME, bytes_accessed=14_000_000, transcendentals=0
        ),
    )(place, first, second, windows)


def on_device(series):
    steps = series.shape[1]
    groups = series.reshape(2, 2, GROUP, steps)
    windows = jnp.stack([groups[:, :, 32 * i : 32 * i + WINDOW] for i in range(8)], axis=2)
    windows = windows.transpose(1, 2, 0, 3, 4).reshape(16, 2 * WINDOW, steps)
    pieces = unpack(lax.all_to_all(pack(windows), ("y", "core"), 0, 0, tiled=True))
    zscore = standardize(pieces.transpose(1, 0, 2).reshape(2 * WINDOW, HALF))

    pair = lax.all_gather(zscore, "zh")
    gathered = lax.all_gather(pair, ("y", "core"))

    offset = WINDOW * lax.axis_index("zh") + lax.rem(lax.axis_index(BULK), 8)
    mine = lax.dynamic_slice_in_dim(pair, offset, SHARE, 1)
    halves = [
        gather_x(lax.all_gather(mine[t], "zl").transpose(1, 0, 2).reshape(SHARE * 4, HALF))
        for t in range(2)
    ]
    return multiply(*halves, gathered).transpose(1, 0, 2)


def solution(mesh):
    split = Mesh(mesh.devices.reshape(SIZES), AXES)
    return jax.shard_map(
        on_device,
        mesh=split,
        in_specs=(P(("x", "zl"), BULK),),
        out_specs=P(None, BULK, ("x", "zl")),
        check_vma=False,
    )
```

```python
import jax
import jax.numpy as jnp
from jax import lax
from jax.experimental import pallas as pl
from jax.experimental.pallas import tpu as pltpu
from jax.sharding import Mesh, PartitionSpec as P

TIME = 3072
HALF = TIME // 2
AXES = ("x", "zl", "zh", "y", "core")
SIZES = (4, 4, 2, 8, 2)
BULK = ("zh", "y", "core")
SHARE = 33
FOUR = 4 * SHARE
WINDOW = 40
ROWS = 1056
GROUP = 8 * SHARE
EDGES = (0, 256, 512, 768, ROWS)

epsilon = 1e-06


def standardize(rows):
    average = jnp.sum(rows, axis=1, keepdims=True) / TIME
    centered = rows - average
    variance = jnp.sum(centered * centered, axis=1, keepdims=True) / TIME
    return (centered * lax.rsqrt(variance + epsilon)).astype(jnp.bfloat16)


def shift(array, axis, by):
    size = lax.axis_size(axis)
    return lax.ppermute(array, axis, [(i, (i + by) % size) for i in range(size)])


def contract(first, second, block, low, high):
    product = 0.0
    for t, part in enumerate((first, second)):
        product += lax.dot_general(
            part[...],
            block[low:high, HALF * t : HALF * t + HALF],
            (((1,), (1,)), ((), ())),
            preferred_element_type=jnp.float32,
        )
    return product * (1.0 / TIME)


def near_kernel(first, second, windows, block, near, held, arrived):
    copies = []
    for group in range(4):
        half, parity = divmod(group, 2)
        copy = pltpu.make_async_copy(
            windows.at[pl.ds(8 * parity, 8), half], held.at[group], arrived.at[group]
        )
        copy.start()
        copies.append(copy)
    for group in range(4):
        copies[group].wait()
        for i in range(8):
            start = GROUP * group + 32 * i
            size = 32 if i < 7 else 40
            block[start : start + size, :] = held[group, i, :size, :]
        low, high = EDGES[group], EDGES[group + 1]
        product = contract(first, second, block, low, high)
        for k in range(3):
            near[k, :, low:high] = product[FOUR * k : FOUR * k + FOUR, :]


def far_kernel(place, first, second, block, near, out, turned):
    for low, high in zip(EDGES[:-1], EDGES[1:]):
        width = high - low
        product = contract(first, second, block, low, high)
        turned[2, :, :width] = product
        for n, k in enumerate((0, 1, 3)):
            turned[k, :, :width] = near[n, :, low:high]
        for x in range(4):
            rows = turned[lax.rem(x - place[0] + 4, 4), :, :width]
            out[:, 4 * x : 4 * x + 4, low:high] = rows.reshape(SHARE, 4, width)


VMEM = pl.BlockSpec(memory_space=pltpu.VMEM)


def multiply_near(first, second, windows):
    rows = first.shape[0]
    return pl.pallas_call(
        near_kernel,
        out_shape=(
            jax.ShapeDtypeStruct((ROWS, TIME), jnp.bfloat16),
            jax.ShapeDtypeStruct((3, FOUR, ROWS), jnp.float32),
        ),
        in_specs=[VMEM, VMEM, pl.BlockSpec(memory_space=pl.ANY)],
        out_specs=(VMEM, VMEM),
        scratch_shapes=[
            pltpu.VMEM((4, 8, WINDOW, TIME), jnp.bfloat16),
            pltpu.SemaphoreType.DMA((4,)),
        ],
        compiler_params=pltpu.CompilerParams(vmem_limit_bytes=48 * 1024 * 1024),
        cost_estimate=pl.CostEstimate(
            flops=2 * rows * ROWS * TIME, bytes_accessed=14_000_000, transcendentals=0
        ),
    )(first, second, windows)


def multiply_far(first, second, block, near):
    place = lax.axis_index("x").astype(jnp.int32).reshape(1)
    return pl.pallas_call(
        far_kernel,
        out_shape=jax.ShapeDtypeStruct((SHARE, 16, ROWS), jnp.float32),
        in_specs=[pl.BlockSpec(memory_space=pltpu.SMEM), VMEM, VMEM, VMEM, VMEM],
        out_specs=VMEM,
        scratch_shapes=[pltpu.VMEM((4, FOUR, 384), jnp.float32)],
        compiler_params=pltpu.CompilerParams(vmem_limit_bytes=12 * 1024 * 1024),
        cost_estimate=pl.CostEstimate(
            flops=2 * FOUR * ROWS * TIME, bytes_accessed=8_000_000, transcendentals=0
        ),
    )(place, first, second, block, near)


def on_device(series):
    groups = series.reshape(4, GROUP, -1)
    windows = jnp.stack([groups[:, 32 * i : 32 * i + WINDOW] for i in range(8)], axis=1)
    windows = windows.reshape(32, WINDOW, -1)
    pieces = lax.all_to_all(windows, BULK, 0, 0, tiled=True)
    window = standardize(pieces.transpose(1, 0, 2).reshape(WINDOW, TIME))
    own = lax.dynamic_slice_in_dim(window, lax.rem(lax.axis_index(BULK), 8), SHARE, 0)
    pair = lax.all_gather(window, "zh")
    gathered = lax.all_gather(pair, ("y", "core"))

    part = lax.all_gather(own, "zl").transpose(1, 0, 2).reshape(FOUR, TIME)
    first, second = part[:, :HALF], part[:, HALF:]
    after_first, before_second = shift(first, "x", 1), shift(second, "x", -1)
    after_second, before_first = shift(second, "x", 1), shift(first, "x", -1)
    far_first, far_second = shift(after_first, "x", 1), shift(before_second, "x", -1)

    near_first = jnp.concatenate([first, before_first, after_first])
    near_second = jnp.concatenate([second, before_second, after_second])
    block, near = multiply_near(near_first, near_second, gathered)
    return multiply_far(far_first, far_second, block, near).transpose(1, 0, 2)


def solution(mesh):
    split = Mesh(mesh.devices.reshape(SIZES), AXES)
    return jax.shard_map(
        on_device,
        mesh=split,
        in_specs=(P(("x", "zl"), BULK),),
        out_specs=P(None, BULK, ("x", "zl")),
        check_vma=False,
    )
```

```python
import jax
import jax.numpy as jnp
from jax import lax
from jax.experimental import pallas as pl
from jax.experimental.pallas import tpu as pltpu
from jax.sharding import Mesh, PartitionSpec as P

TIME = 3072
HALF = TIME // 2
AXES = ("x", "zl", "zh", "y", "core")
SIZES = (4, 4, 2, 8, 2)
BULK = ("zh", "y", "core")
SHARE = 33
FOUR = 4 * SHARE
SLOT = 144
WINDOW = 40
ROWS = 1056
GROUP = 8 * SHARE
EDGES = (0, 256, 512, 768, ROWS)

epsilon = 1e-06


def standardize(rows):
    average = jnp.sum(rows, axis=1, keepdims=True) / TIME
    centered = rows - average
    variance = jnp.sum(centered * centered, axis=1, keepdims=True) / TIME
    return (centered * lax.rsqrt(variance + epsilon)).astype(jnp.bfloat16)


def shift(array, axis, by):
    size = lax.axis_size(axis)
    return lax.ppermute(array, axis, [(i, (i + by) % size) for i in range(size)])


def contract(first, second, block, low, high):
    product = 0.0
    for t, part in enumerate((first, second)):
        product += lax.dot_general(
            part[...],
            block[low:high, HALF * t : HALF * t + HALF],
            (((1,), (1,)), ((), ())),
            preferred_element_type=jnp.float32,
        )
    return product * (1.0 / TIME)


def near_kernel(*refs):
    pieces, (windows, block, near, held, parts, arrived) = refs[:6], refs[6:]
    copies = []
    for group in range(4):
        half, parity = divmod(group, 2)
        copy = pltpu.make_async_copy(
            windows.at[pl.ds(8 * parity, 8), half], held.at[group], arrived.at[group]
        )
        copy.start()
        copies.append(copy)
    for t in range(2):
        for k in range(3):
            parts[t, SLOT * k : SLOT * k + FOUR, :] = pieces[3 * t + k][...]
    for group in range(4):
        copies[group].wait()
        for i in range(8):
            start = GROUP * group + 32 * i
            size = 32 if i < 7 else 40
            block[start : start + size, :] = held[group, i, :size, :]
        low, high = EDGES[group], EDGES[group + 1]
        product = contract(parts.at[0], parts.at[1], block, low, high)
        for k in range(3):
            near[k, :, low:high] = product[SLOT * k : SLOT * k + FOUR, :]


def far_kernel(place, first, second, block, near, out, turned):
    for low, high in zip(EDGES[:-1], EDGES[1:]):
        width = high - low
        product = contract(first, second, block, low, high)
        turned[2, :, :width] = product
        for n, k in enumerate((0, 1, 3)):
            turned[k, :, :width] = near[n, :, low:high]
        for x in range(4):
            rows = turned[lax.rem(x - place[0] + 4, 4), :, :width]
            out[:, 4 * x : 4 * x + 4, low:high] = rows.reshape(SHARE, 4, width)


VMEM = pl.BlockSpec(memory_space=pltpu.VMEM)


def multiply_near(pieces, windows):
    return pl.pallas_call(
        near_kernel,
        out_shape=(
            jax.ShapeDtypeStruct((ROWS, TIME), jnp.bfloat16),
            jax.ShapeDtypeStruct((3, FOUR, ROWS), jnp.float32),
        ),
        in_specs=[VMEM] * 6 + [pl.BlockSpec(memory_space=pl.ANY)],
        out_specs=(VMEM, VMEM),
        scratch_shapes=[
            pltpu.VMEM((4, 8, WINDOW, TIME), jnp.bfloat16),
            pltpu.VMEM((2, 3 * SLOT, HALF), jnp.bfloat16),
            pltpu.SemaphoreType.DMA((4,)),
        ],
        compiler_params=pltpu.CompilerParams(vmem_limit_bytes=40 * 1024 * 1024),
        cost_estimate=pl.CostEstimate(
            flops=6 * FOUR * ROWS * TIME, bytes_accessed=14_000_000, transcendentals=0
        ),
    )(*pieces, windows)


def multiply_far(first, second, block, near):
    place = lax.axis_index("x").astype(jnp.int32).reshape(1)
    return pl.pallas_call(
        far_kernel,
        out_shape=jax.ShapeDtypeStruct((SHARE, 16, ROWS), jnp.float32),
        in_specs=[pl.BlockSpec(memory_space=pltpu.SMEM), VMEM, VMEM, VMEM, VMEM],
        out_specs=VMEM,
        scratch_shapes=[pltpu.VMEM((4, FOUR, 384), jnp.float32)],
        compiler_params=pltpu.CompilerParams(vmem_limit_bytes=24 * 1024 * 1024),
        cost_estimate=pl.CostEstimate(
            flops=2 * FOUR * ROWS * TIME, bytes_accessed=8_000_000, transcendentals=0
        ),
    )(place, first, second, block, near)


def on_device(series):
    groups = series.reshape(4, GROUP, -1)
    windows = jnp.stack([groups[:, 32 * i : 32 * i + WINDOW] for i in range(8)], axis=1)
    windows = windows.reshape(32, WINDOW, -1)
    pieces = lax.all_to_all(windows, BULK, 0, 0, tiled=True)
    window = standardize(pieces.transpose(1, 0, 2).reshape(WINDOW, TIME))
    own = lax.dynamic_slice_in_dim(window, lax.rem(lax.axis_index(BULK), 8), SHARE, 0)
    pair = lax.all_gather(window, "zh")
    gathered = lax.all_gather(pair, ("y", "core"))

    part = lax.all_gather(own, "zl").transpose(1, 0, 2).reshape(FOUR, TIME)
    first, second = part[:, :HALF], part[:, HALF:]
    after_first, before_second = shift(first, "x", 1), shift(second, "x", -1)
    after_second, before_first = shift(second, "x", 1), shift(first, "x", -1)
    far_first, far_second = shift(after_first, "x", 1), shift(before_second, "x", -1)

    pieces = (first, before_first, after_first, second, before_second, after_second)
    block, near = multiply_near(pieces, gathered)
    return multiply_far(far_first, far_second, block, near).transpose(1, 0, 2)


def solution(mesh):
    split = Mesh(mesh.devices.reshape(SIZES), AXES)
    return jax.shard_map(
        on_device,
        mesh=split,
        in_specs=(P(("x", "zl"), BULK),),
        out_specs=P(None, BULK, ("x", "zl")),
        check_vma=False,
    )
```

```python
import jax
import jax.numpy as jnp
from jax import lax
from jax.experimental import pallas as pl
from jax.experimental.pallas import tpu as pltpu
from jax.sharding import Mesh, PartitionSpec as P

TIME = 3072
HALF = TIME // 2
AXES = ("x", "zl", "zh", "y", "core")
SIZES = (4, 4, 2, 8, 2)
BULK = ("zh", "y", "core")
SHARE = 33
FOUR = 4 * SHARE
SLOT = 144
WINDOW = 40
WIDE = TIME + 128
ROWS = 1056
GROUP = 8 * SHARE
EDGES = (0, 256, 512, 768, ROWS)

epsilon = 1e-06


def standardize(rows):
    axes = tuple(range(1, rows.ndim))
    average = jnp.sum(rows, axis=axes, keepdims=True) / TIME
    centered = rows - average
    variance = jnp.sum(centered * centered, axis=axes, keepdims=True) / TIME
    return (centered * lax.rsqrt(variance + epsilon)).astype(jnp.bfloat16)


def pack(series):
    groups = series.reshape(4, GROUP, 96)
    windows = jnp.stack([groups[:, 32 * i : 32 * i + WINDOW] for i in range(8)], axis=1)
    windows = windows.reshape(32, WINDOW, 96)
    single = groups[:, 256:].reshape(32, 1, 96)
    cuts = [slice(32 * p, 32 * p + 32) for p in range(3)]
    side = [windows[:, 32:, cut] for cut in cuts] + [single[:, :, cut] for cut in cuts]
    side = jnp.concatenate(side + [jnp.zeros((32, 5, 32), series.dtype)], axis=1)
    return jnp.concatenate([windows[:, :32], side], axis=2)


def unpack(pieces):
    side = pieces[:, :, 96:]
    last = jnp.concatenate([side[:, 8 * p : 8 * p + 8] for p in range(3)], axis=2)
    window = jnp.concatenate([pieces[:, :, :96], last], axis=1)
    single = jnp.concatenate([side[:, 24 + p] for p in range(3)], axis=1)
    return window.transpose(1, 0, 2).reshape(WINDOW, TIME), single[None]


def shift(array, axis, by):
    size = lax.axis_size(axis)
    return lax.ppermute(array, axis, [(i, (i + by) % size) for i in range(size)])


def contract(first, second, block, low, high):
    product = 0.0
    for t, part in enumerate((first, second)):
        product += lax.dot_general(
            part[...],
            block[low:high, HALF * t : HALF * t + HALF],
            (((1,), (1,)), ((), ())),
            preferred_element_type=jnp.float32,
        )
    return product * (1.0 / TIME)


def near_kernel(*refs):
    pieces, (windows, block, near, held, parts, singles, tail, arrived) = refs[:6], refs[6:]
    copies = []
    for group in range(4):
        half, parity = divmod(group, 2)
        copy = pltpu.make_async_copy(
            windows.at[pl.ds(8 * parity, 8), half], held.at[group], arrived.at[group]
        )
        copy.start()
        copies.append(copy)
    for t in range(2):
        for k in range(3):
            parts[t, SLOT * k : SLOT * k + FOUR, :] = pieces[3 * t + k][...]
    for group in range(4):
        copies[group].wait()
        for i in range(8):
            start = GROUP * group + 32 * i
            block[start : start + 32, :] = held[group, i, :, :TIME]
            singles[32 * i : 32 * i + 32, :] = held[group, i, :, TIME:].astype(jnp.float32)
        for source in range(32):
            steps = singles[pl.ds(source, 8, stride=32), :]
            tail[:, 96 * source : 96 * source + 96] = steps[:, :96]
        start = GROUP * group + 256
        block[start : start + 8, :] = tail[...].astype(jnp.bfloat16)
        low, high = EDGES[group], EDGES[group + 1]
        product = contract(parts.at[0], parts.at[1], block, low, high)
        for k in range(3):
            near[k, :, low:high] = product[SLOT * k : SLOT * k + FOUR, :]


def far_kernel(place, first, second, block, near, out, turned):
    for low, high in zip(EDGES[:-1], EDGES[1:]):
        width = high - low
        product = contract(first, second, block, low, high)
        turned[2, :, :width] = product
        for n, k in enumerate((0, 1, 3)):
            turned[k, :, :width] = near[n, :, low:high]
        for x in range(4):
            rows = turned[lax.rem(x - place[0] + 4, 4), :, :width]
            out[:, 4 * x : 4 * x + 4, low:high] = rows.reshape(SHARE, 4, width)


VMEM = pl.BlockSpec(memory_space=pltpu.VMEM)


def multiply_near(pieces, windows):
    return pl.pallas_call(
        near_kernel,
        out_shape=(
            jax.ShapeDtypeStruct((ROWS, TIME), jnp.bfloat16),
            jax.ShapeDtypeStruct((3, FOUR, ROWS), jnp.float32),
        ),
        in_specs=[VMEM] * 6 + [pl.BlockSpec(memory_space=pl.ANY)],
        out_specs=(VMEM, VMEM),
        scratch_shapes=[
            pltpu.VMEM((4, 8, 32, WIDE), jnp.bfloat16),
            pltpu.VMEM((2, 3 * SLOT, HALF), jnp.bfloat16),
            pltpu.VMEM((256, 128), jnp.float32),
            pltpu.VMEM((8, TIME), jnp.float32),
            pltpu.SemaphoreType.DMA((4,)),
        ],
        compiler_params=pltpu.CompilerParams(vmem_limit_bytes=40 * 1024 * 1024),
        cost_estimate=pl.CostEstimate(
            flops=6 * FOUR * ROWS * TIME, bytes_accessed=14_000_000, transcendentals=0
        ),
    )(*pieces, windows)


def multiply_far(first, second, block, near):
    place = lax.axis_index("x").astype(jnp.int32).reshape(1)
    return pl.pallas_call(
        far_kernel,
        out_shape=jax.ShapeDtypeStruct((SHARE, 16, ROWS), jnp.float32),
        in_specs=[pl.BlockSpec(memory_space=pltpu.SMEM), VMEM, VMEM, VMEM, VMEM],
        out_specs=VMEM,
        scratch_shapes=[pltpu.VMEM((4, FOUR, 384), jnp.float32)],
        compiler_params=pltpu.CompilerParams(vmem_limit_bytes=24 * 1024 * 1024),
        cost_estimate=pl.CostEstimate(
            flops=2 * FOUR * ROWS * TIME, bytes_accessed=8_000_000, transcendentals=0
        ),
    )(place, first, second, block, near)


def on_device(series):
    window, single = unpack(lax.all_to_all(pack(series), BULK, 0, 0, tiled=True))
    window, single = standardize(window), standardize(single)
    own = lax.dynamic_slice_in_dim(window, lax.rem(lax.axis_index(BULK), 8), SHARE, 0)
    wide = jnp.concatenate([window[:32], jnp.pad(single[0], ((0, 0), (0, 32)))], axis=1)
    gathered = lax.all_gather(lax.all_gather(wide, "zh"), ("y", "core"))

    part = lax.all_gather(own, "zl").transpose(1, 0, 2).reshape(FOUR, TIME)
    first, second = part[:, :HALF], part[:, HALF:]
    after_first, before_second = shift(first, "x", 1), shift(second, "x", -1)
    after_second, before_first = shift(second, "x", 1), shift(first, "x", -1)
    far_first, far_second = shift(after_first, "x", 1), shift(before_second, "x", -1)

    pieces = (first, before_first, after_first, second, before_second, after_second)
    block, near = multiply_near(pieces, gathered)
    return multiply_far(far_first, far_second, block, near).transpose(1, 0, 2)


def solution(mesh):
    split = Mesh(mesh.devices.reshape(SIZES), AXES)
    return jax.shard_map(
        on_device,
        mesh=split,
        in_specs=(P(("x", "zl"), BULK),),
        out_specs=P(None, BULK, ("x", "zl")),
        check_vma=False,
    )
```

```python
import jax
import jax.numpy as jnp
from jax import lax
from jax.experimental import pallas as pl
from jax.experimental.pallas import tpu as pltpu
from jax.sharding import Mesh, PartitionSpec as P

TIME = 3072
HALF = TIME // 2
AXES = ("x", "zl", "zh", "y", "core")
SIZES = (4, 4, 2, 8, 2)
BULK = ("zh", "y", "core")
SHARE = 33
FOUR = 4 * SHARE
SLOT = 144
WINDOW = 40
WIDE = TIME + 128
ROWS = 1056
GROUP = 8 * SHARE
EDGES = (0, 256, 512, 768, ROWS)

VMEM = pl.BlockSpec(memory_space=pltpu.VMEM)

epsilon = 1e-06


def standardize(rows, axes):
    average = jnp.sum(rows, axis=axes, keepdims=True) / TIME
    centered = rows - average
    variance = jnp.sum(centered * centered, axis=axes, keepdims=True) / TIME
    return (centered * lax.rsqrt(variance + epsilon)).astype(jnp.bfloat16)


def standardize_kernel(pieces, window, wide, rows, single):
    for source in range(32):
        start = 96 * source
        rows[:32, start : start + 96] = pieces[source, :, :96]
        for p in range(3):
            cut = slice(start + 32 * p, start + 32 * p + 32)
            rows[32:, cut] = pieces[source, 8 * p : 8 * p + 8, 96:]
            single[source : source + 1, 32 * p : 32 * p + 32] = pieces[
                source, 24 + p : 25 + p, 96:
            ]
    scores = standardize(rows[...], (1,))
    window[...] = scores
    wide[:, :TIME] = scores[:32]
    wide[:, TIME:] = jnp.zeros((32, 128), jnp.bfloat16)
    wide[:, TIME : TIME + 96] = standardize(single[:, :96], (0, 1))


def standardize_pieces(pieces):
    return pl.pallas_call(
        standardize_kernel,
        out_shape=(
            jax.ShapeDtypeStruct((WINDOW, TIME), jnp.bfloat16),
            jax.ShapeDtypeStruct((32, WIDE), jnp.bfloat16),
        ),
        in_specs=[VMEM],
        out_specs=(VMEM, VMEM),
        scratch_shapes=[
            pltpu.VMEM((WINDOW, TIME), jnp.float32),
            pltpu.VMEM((32, 128), jnp.float32),
        ],
        compiler_params=pltpu.CompilerParams(vmem_limit_bytes=8 * 1024 * 1024),
    )(pieces)


def pack(series):
    groups = series.reshape(4, GROUP, 96)
    windows = jnp.stack([groups[:, 32 * i : 32 * i + WINDOW] for i in range(8)], axis=1)
    windows = windows.reshape(32, WINDOW, 96)
    single = groups[:, 256:].reshape(32, 1, 96)
    cuts = [slice(32 * p, 32 * p + 32) for p in range(3)]
    side = [windows[:, 32:, cut] for cut in cuts] + [single[:, :, cut] for cut in cuts]
    side = jnp.concatenate(side + [jnp.zeros((32, 5, 32), series.dtype)], axis=1)
    return jnp.concatenate([windows[:, :32], side], axis=2)


def shift(array, axis, by):
    size = lax.axis_size(axis)
    return lax.ppermute(array, axis, [(i, (i + by) % size) for i in range(size)])


def contract(first, second, block, low, high):
    product = 0.0
    for t, part in enumerate((first, second)):
        product += lax.dot_general(
            part[...],
            block[low:high, HALF * t : HALF * t + HALF],
            (((1,), (1,)), ((), ())),
            preferred_element_type=jnp.float32,
        )
    return product * (1.0 / TIME)


def near_kernel(*refs):
    pieces, (windows, block, near, held, parts, singles, tail, arrived) = refs[:6], refs[6:]
    copies = []
    for group in range(4):
        half, parity = divmod(group, 2)
        copy = pltpu.make_async_copy(
            windows.at[pl.ds(8 * parity, 8), half], held.at[group], arrived.at[group]
        )
        copy.start()
        copies.append(copy)
    for t in range(2):
        for k in range(3):
            parts[t, SLOT * k : SLOT * k + FOUR, :] = pieces[3 * t + k][...]
    for group in range(4):
        copies[group].wait()
        for i in range(8):
            start = GROUP * group + 32 * i
            block[start : start + 32, :] = held[group, i, :, :TIME]
            singles[32 * i : 32 * i + 32, :] = held[group, i, :, TIME:].astype(jnp.float32)
        for source in range(32):
            steps = singles[pl.ds(source, 8, stride=32), :]
            tail[:, 96 * source : 96 * source + 96] = steps[:, :96]
        start = GROUP * group + 256
        block[start : start + 8, :] = tail[...].astype(jnp.bfloat16)
        low, high = EDGES[group], EDGES[group + 1]
        product = contract(parts.at[0], parts.at[1], block, low, high)
        for k in range(3):
            near[k, :, low:high] = product[SLOT * k : SLOT * k + FOUR, :]


def far_kernel(place, first, second, block, near, out, turned):
    for low, high in zip(EDGES[:-1], EDGES[1:]):
        width = high - low
        product = contract(first, second, block, low, high)
        turned[2, :, :width] = product
        for n, k in enumerate((0, 1, 3)):
            turned[k, :, :width] = near[n, :, low:high]
        for x in range(4):
            rows = turned[lax.rem(x - place[0] + 4, 4), :, :width]
            out[:, 4 * x : 4 * x + 4, low:high] = rows.reshape(SHARE, 4, width)


def multiply_near(pieces, windows):
    return pl.pallas_call(
        near_kernel,
        out_shape=(
            jax.ShapeDtypeStruct((ROWS, TIME), jnp.bfloat16),
            jax.ShapeDtypeStruct((3, FOUR, ROWS), jnp.float32),
        ),
        in_specs=[VMEM] * 6 + [pl.BlockSpec(memory_space=pl.ANY)],
        out_specs=(VMEM, VMEM),
        scratch_shapes=[
            pltpu.VMEM((4, 8, 32, WIDE), jnp.bfloat16),
            pltpu.VMEM((2, 3 * SLOT, HALF), jnp.bfloat16),
            pltpu.VMEM((256, 128), jnp.float32),
            pltpu.VMEM((8, TIME), jnp.float32),
            pltpu.SemaphoreType.DMA((4,)),
        ],
        compiler_params=pltpu.CompilerParams(vmem_limit_bytes=40 * 1024 * 1024),
        cost_estimate=pl.CostEstimate(
            flops=6 * FOUR * ROWS * TIME, bytes_accessed=14_000_000, transcendentals=0
        ),
    )(*pieces, windows)


def multiply_far(first, second, block, near):
    place = lax.axis_index("x").astype(jnp.int32).reshape(1)
    return pl.pallas_call(
        far_kernel,
        out_shape=jax.ShapeDtypeStruct((SHARE, 16, ROWS), jnp.float32),
        in_specs=[pl.BlockSpec(memory_space=pltpu.SMEM), VMEM, VMEM, VMEM, VMEM],
        out_specs=VMEM,
        scratch_shapes=[pltpu.VMEM((4, FOUR, 384), jnp.float32)],
        compiler_params=pltpu.CompilerParams(vmem_limit_bytes=24 * 1024 * 1024),
        cost_estimate=pl.CostEstimate(
            flops=2 * FOUR * ROWS * TIME, bytes_accessed=8_000_000, transcendentals=0
        ),
    )(place, first, second, block, near)


def on_device(series):
    window, wide = standardize_pieces(lax.all_to_all(pack(series), BULK, 0, 0, tiled=True))
    own = lax.dynamic_slice_in_dim(window, lax.rem(lax.axis_index(BULK), 8), SHARE, 0)
    gathered = lax.all_gather(lax.all_gather(wide, "zh"), ("y", "core"))

    part = lax.all_gather(own, "zl").transpose(1, 0, 2).reshape(FOUR, TIME)
    first, second = part[:, :HALF], part[:, HALF:]
    after_first, before_second = shift(first, "x", 1), shift(second, "x", -1)
    after_second, before_first = shift(second, "x", 1), shift(first, "x", -1)
    far_first, far_second = shift(after_first, "x", 1), shift(before_second, "x", -1)

    pieces = (first, before_first, after_first, second, before_second, after_second)
    block, near = multiply_near(pieces, gathered)
    return multiply_far(far_first, far_second, block, near).transpose(1, 0, 2)


def solution(mesh):
    split = Mesh(mesh.devices.reshape(SIZES), AXES)
    return jax.shard_map(
        on_device,
        mesh=split,
        in_specs=(P(("x", "zl"), BULK),),
        out_specs=P(None, BULK, ("x", "zl")),
        check_vma=False,
    )
```

```python
import jax
import jax.numpy as jnp
from jax import lax
from jax.experimental import pallas as pl
from jax.experimental.pallas import tpu as pltpu
from jax.sharding import Mesh, PartitionSpec as P

TIME = 3072
HALF = TIME // 2
AXES = ("x", "zl", "zh", "y", "core")
SIZES = (4, 4, 2, 8, 2)
BULK = ("zh", "y", "core")
SHARE = 33
FOUR = 4 * SHARE
SLOT = 144
WINDOW = 40
WIDE = TIME + 128
ROWS = 1056
GROUP = 8 * SHARE
EDGES = (0, 256, 512, 768, ROWS)

VMEM = pl.BlockSpec(memory_space=pltpu.VMEM)

epsilon = 1e-06


def standardize(rows, axes):
    average = jnp.sum(rows, axis=axes, keepdims=True) / TIME
    centered = rows - average
    variance = jnp.sum(centered * centered, axis=axes, keepdims=True) / TIME
    return (centered * lax.rsqrt(variance + epsilon)).astype(jnp.bfloat16)


def standardize_kernel(pieces, window, wide, rows, single):
    for source in range(32):
        start = 96 * source
        rows[:32, start : start + 96] = pieces[source, :, :96]
        for p in range(3):
            cut = slice(start + 32 * p, start + 32 * p + 32)
            rows[32:, cut] = pieces[source, 8 * p : 8 * p + 8, 96:]
            single[source : source + 1, 32 * p : 32 * p + 32] = pieces[
                source, 24 + p : 25 + p, 96:
            ]
    scores = standardize(rows[...], (1,))
    window[...] = scores
    wide[:, :TIME] = scores[:32]
    wide[:, TIME:] = jnp.zeros((32, 128), jnp.bfloat16)
    wide[:, TIME : TIME + 96] = standardize(single[:, :96], (0, 1))


def standardize_pieces(pieces):
    return pl.pallas_call(
        standardize_kernel,
        out_shape=(
            jax.ShapeDtypeStruct((WINDOW, TIME), jnp.bfloat16),
            jax.ShapeDtypeStruct((32, WIDE), jnp.bfloat16),
        ),
        in_specs=[VMEM],
        out_specs=(VMEM, VMEM),
        scratch_shapes=[
            pltpu.VMEM((WINDOW, TIME), jnp.float32),
            pltpu.VMEM((32, 128), jnp.float32),
        ],
        compiler_params=pltpu.CompilerParams(vmem_limit_bytes=8 * 1024 * 1024),
    )(pieces)


def pack_kernel(steps, packed, rows):
    rows[...] = steps[...].T
    for device in range(32):
        group, i = divmod(device, 8)
        start, single = GROUP * group + 32 * i, GROUP * group + 256 + i
        packed[device, :, :96] = rows[start : start + 32, :]
        for p in range(3):
            cut = slice(32 * p, 32 * p + 32)
            packed[device, 8 * p : 8 * p + 8, 96:] = rows[start + 32 : start + 40, cut]
            packed[device, 24 + p : 25 + p, 96:] = rows[single : single + 1, cut]
        packed[device, 27:, 96:] = jnp.zeros((5, 32), jnp.float32)


def pack(series):
    return pl.pallas_call(
        pack_kernel,
        out_shape=jax.ShapeDtypeStruct((32, 32, 128), jnp.float32),
        in_specs=[VMEM],
        out_specs=VMEM,
        scratch_shapes=[pltpu.VMEM((ROWS, 96), jnp.float32)],
        compiler_params=pltpu.CompilerParams(vmem_limit_bytes=8 * 1024 * 1024),
    )(series.T)


def shift(array, axis, by):
    size = lax.axis_size(axis)
    return lax.ppermute(array, axis, [(i, (i + by) % size) for i in range(size)])


def contract(first, second, block, low, high):
    product = 0.0
    for t, part in enumerate((first, second)):
        product += lax.dot_general(
            part[...],
            block[low:high, HALF * t : HALF * t + HALF],
            (((1,), (1,)), ((), ())),
            preferred_element_type=jnp.float32,
        )
    return product * (1.0 / TIME)


def near_kernel(*refs):
    pieces, (windows, block, near, held, parts, singles, tail, arrived) = refs[:6], refs[6:]
    copies = []
    for group in range(4):
        half, parity = divmod(group, 2)
        copy = pltpu.make_async_copy(
            windows.at[pl.ds(8 * parity, 8), half], held.at[group], arrived.at[group]
        )
        copy.start()
        copies.append(copy)
    for t in range(2):
        for k in range(3):
            parts[t, SLOT * k : SLOT * k + FOUR, :] = pieces[3 * t + k][...]
    for copy in copies:
        copy.wait()
    for group in range(4):
        for i in range(8):
            start = GROUP * group + 32 * i
            block[start : start + 32, :] = held[group, i, :, :TIME]
            singles[32 * i : 32 * i + 32, :] = held[group, i, :, TIME:].astype(jnp.float32)
        for source in range(32):
            steps = singles[pl.ds(source, 8, stride=32), :]
            tail[:, 96 * source : 96 * source + 96] = steps[:, :96]
        start = GROUP * group + 256
        block[start : start + 8, :] = tail[...].astype(jnp.bfloat16)
    for low, high in zip(EDGES[:-1], EDGES[1:]):
        product = contract(parts.at[0], parts.at[1], block, low, high)
        for k in range(3):
            near[k, :, low:high] = product[SLOT * k : SLOT * k + FOUR, :]


def far_kernel(place, first, second, block, near, out, turned, ready, sent):
    copies = []
    for tile, (low, high) in enumerate(zip(EDGES[:-1], EDGES[1:])):
        width = high - low
        product = contract(first, second, block, low, high)
        turned[2, :, :width] = product
        for n, k in enumerate((0, 1, 3)):
            turned[k, :, :width] = near[n, :, low:high]
        for x in range(4):
            rows = turned[lax.rem(x - place[0] + 4, 4), :, :width]
            ready[:, 4 * x : 4 * x + 4, low:high] = rows.reshape(SHARE, 4, width)
        done = slice(low, high)
        copy = pltpu.make_async_copy(ready.at[:, :, done], out.at[:, :, done], sent.at[tile])
        copy.start()
        copies.append(copy)
    for copy in copies:
        copy.wait()


def multiply_near(pieces, windows):
    return pl.pallas_call(
        near_kernel,
        out_shape=(
            jax.ShapeDtypeStruct((ROWS, TIME), jnp.bfloat16),
            jax.ShapeDtypeStruct((3, FOUR, ROWS), jnp.float32),
        ),
        in_specs=[VMEM] * 6 + [pl.BlockSpec(memory_space=pl.ANY)],
        out_specs=(VMEM, VMEM),
        scratch_shapes=[
            pltpu.VMEM((4, 8, 32, WIDE), jnp.bfloat16),
            pltpu.VMEM((2, 3 * SLOT, HALF), jnp.bfloat16),
            pltpu.VMEM((256, 128), jnp.float32),
            pltpu.VMEM((8, TIME), jnp.float32),
            pltpu.SemaphoreType.DMA((4,)),
        ],
        compiler_params=pltpu.CompilerParams(vmem_limit_bytes=40 * 1024 * 1024),
        cost_estimate=pl.CostEstimate(
            flops=6 * FOUR * ROWS * TIME, bytes_accessed=14_000_000, transcendentals=0
        ),
    )(*pieces, windows)


def multiply_far(first, second, block, near):
    place = lax.axis_index("x").astype(jnp.int32).reshape(1)
    return pl.pallas_call(
        far_kernel,
        out_shape=jax.ShapeDtypeStruct((SHARE, 16, ROWS), jnp.float32),
        in_specs=[pl.BlockSpec(memory_space=pltpu.SMEM), VMEM, VMEM, VMEM, VMEM],
        out_specs=pl.BlockSpec(memory_space=pl.ANY),
        scratch_shapes=[
            pltpu.VMEM((4, FOUR, 384), jnp.float32),
            pltpu.VMEM((SHARE, 16, ROWS), jnp.float32),
            pltpu.SemaphoreType.DMA((4,)),
        ],
        compiler_params=pltpu.CompilerParams(vmem_limit_bytes=24 * 1024 * 1024),
        cost_estimate=pl.CostEstimate(
            flops=2 * FOUR * ROWS * TIME, bytes_accessed=8_000_000, transcendentals=0
        ),
    )(place, first, second, block, near)


def on_device(series):
    window, wide = standardize_pieces(lax.all_to_all(pack(series), BULK, 0, 0, tiled=True))
    own = lax.dynamic_slice_in_dim(window, lax.rem(lax.axis_index(BULK), 8), SHARE, 0)
    gathered = lax.all_gather(lax.all_gather(wide, "zh"), ("y", "core"))

    part = lax.all_gather(own.reshape(SHARE, TIME // 128, 128), "zl")
    part = part.transpose(1, 0, 2, 3).reshape(FOUR, TIME)
    first, second = part[:, :HALF], part[:, HALF:]
    after_first, before_second = shift(first, "x", 1), shift(second, "x", -1)
    after_second, before_first = shift(second, "x", 1), shift(first, "x", -1)
    far_first, far_second = shift(after_first, "x", 1), shift(before_second, "x", -1)

    pieces = (first, before_first, after_first, second, before_second, after_second)
    block, near = multiply_near(pieces, gathered)
    return multiply_far(far_first, far_second, block, near).transpose(1, 0, 2)


def solution(mesh):
    split = Mesh(mesh.devices.reshape(SIZES), AXES)
    return jax.shard_map(
        on_device,
        mesh=split,
        in_specs=(P(("x", "zl"), BULK),),
        out_specs=P(None, BULK, ("x", "zl")),
        check_vma=False,
    )
```

```python
import jax
import jax.numpy as jnp
from jax import lax
from jax.experimental import pallas as pl
from jax.experimental.pallas import tpu as pltpu
from jax.sharding import Mesh, PartitionSpec as P

TIME = 3072
HALF = TIME // 2
AXES = ("x", "zl", "zh", "y", "core")
SIZES = (4, 4, 2, 8, 2)
BULK = ("zh", "y", "core")
SHARE = 33
FOUR = 4 * SHARE
SLOT = 144
WINDOW = 40
WIDE = TIME + 128
ROWS = 1056
GROUP = 8 * SHARE
EDGES = (0, 256, 512, 768, ROWS)

VMEM = pl.BlockSpec(memory_space=pltpu.VMEM)

epsilon = 1e-06


def standardize(rows, axes):
    average = jnp.sum(rows, axis=axes, keepdims=True) / TIME
    centered = rows - average
    variance = jnp.sum(centered * centered, axis=axes, keepdims=True) / TIME
    return (centered * lax.rsqrt(variance + epsilon)).astype(jnp.bfloat16)


def standardize_kernel(pieces, window, wide, rows, single):
    for source in range(32):
        start = 96 * source
        rows[:32, start : start + 96] = pieces[source, :, :96]
        for p in range(3):
            cut = slice(start + 32 * p, start + 32 * p + 32)
            rows[32:, cut] = pieces[source, 8 * p : 8 * p + 8, 96:]
            single[source : source + 1, 32 * p : 32 * p + 32] = pieces[
                source, 24 + p : 25 + p, 96:
            ]
    scores = standardize(rows[...], (1,))
    window[...] = scores
    wide[:, :TIME] = scores[:32]
    wide[:, TIME:] = jnp.zeros((32, 128), jnp.bfloat16)
    wide[:, TIME : TIME + 96] = standardize(single[:, :96], (0, 1))


def standardize_pieces(pieces):
    return pl.pallas_call(
        standardize_kernel,
        out_shape=(
            jax.ShapeDtypeStruct((WINDOW, TIME), jnp.bfloat16),
            jax.ShapeDtypeStruct((32, WIDE), jnp.bfloat16),
        ),
        in_specs=[VMEM],
        out_specs=(VMEM, VMEM),
        scratch_shapes=[
            pltpu.VMEM((WINDOW, TIME), jnp.float32),
            pltpu.VMEM((32, 128), jnp.float32),
        ],
        compiler_params=pltpu.CompilerParams(vmem_limit_bytes=8 * 1024 * 1024),
    )(pieces)


def pack_kernel(steps, packed, rows):
    rows[...] = steps[...].T
    for device in range(32):
        group, i = divmod(device, 8)
        start, single = GROUP * group + 32 * i, GROUP * group + 256 + i
        packed[device, :, :96] = rows[start : start + 32, :]
        for p in range(3):
            cut = slice(32 * p, 32 * p + 32)
            packed[device, 8 * p : 8 * p + 8, 96:] = rows[start + 32 : start + 40, cut]
            packed[device, 24 + p : 25 + p, 96:] = rows[single : single + 1, cut]
        packed[device, 27:, 96:] = jnp.zeros((5, 32), jnp.float32)


def pack(series):
    return pl.pallas_call(
        pack_kernel,
        out_shape=jax.ShapeDtypeStruct((32, 32, 128), jnp.float32),
        in_specs=[VMEM],
        out_specs=VMEM,
        scratch_shapes=[pltpu.VMEM((ROWS, 96), jnp.float32)],
        compiler_params=pltpu.CompilerParams(vmem_limit_bytes=8 * 1024 * 1024),
    )(series.T)


def shift(array, axis, by):
    size = lax.axis_size(axis)
    return lax.ppermute(array, axis, [(i, (i + by) % size) for i in range(size)])


def contract(first, second, block, low, high):
    product = 0.0
    for t, part in enumerate((first, second)):
        product += lax.dot_general(
            part[...],
            block[low:high, HALF * t : HALF * t + HALF],
            (((1,), (1,)), ((), ())),
            preferred_element_type=jnp.float32,
        )
    return product * (1.0 / TIME)


def order_kernel(windows, block, held, singles, tail, arrived):
    copies = []
    for group in range(4):
        half, parity = divmod(group, 2)
        copy = pltpu.make_async_copy(
            windows.at[pl.ds(8 * parity, 8), half], held.at[group], arrived.at[group]
        )
        copy.start()
        copies.append(copy)
    for group in range(4):
        copies[group].wait()
        for i in range(8):
            start = GROUP * group + 32 * i
            block[start : start + 32, :] = held[group, i, :, :TIME]
            singles[32 * i : 32 * i + 32, :] = held[group, i, :, TIME:].astype(jnp.float32)
        for source in range(32):
            steps = singles[pl.ds(source, 8, stride=32), :]
            tail[:, 96 * source : 96 * source + 96] = steps[:, :96]
        start = GROUP * group + 256
        block[start : start + 8, :] = tail[...].astype(jnp.bfloat16)


def order(windows):
    return pl.pallas_call(
        order_kernel,
        out_shape=jax.ShapeDtypeStruct((ROWS, TIME), jnp.bfloat16),
        in_specs=[pl.BlockSpec(memory_space=pl.ANY)],
        out_specs=VMEM,
        scratch_shapes=[
            pltpu.VMEM((4, 8, 32, WIDE), jnp.bfloat16),
            pltpu.VMEM((256, 128), jnp.float32),
            pltpu.VMEM((8, TIME), jnp.float32),
            pltpu.SemaphoreType.DMA((4,)),
        ],
        compiler_params=pltpu.CompilerParams(vmem_limit_bytes=44 * 1024 * 1024),
        cost_estimate=pl.CostEstimate(flops=0, bytes_accessed=7_000_000, transcendentals=0),
    )(windows)


def product_kernel(place, *refs):
    pieces, (block, out, parts, turned, ready, sent) = refs[:8], refs[8:]
    for t in range(2):
        for k in range(4):
            parts[t, SLOT * k : SLOT * k + FOUR, :] = pieces[4 * t + k][...]
    copies = []
    for tile, (low, high) in enumerate(zip(EDGES[:-1], EDGES[1:])):
        width = high - low
        product = contract(parts.at[0], parts.at[1], block, low, high)
        for k in range(4):
            turned[k, :, :width] = product[SLOT * k : SLOT * k + FOUR, :]
        for x in range(4):
            rows = turned[lax.rem(x - place[0] + 4, 4), :, :width]
            ready[:, 4 * x : 4 * x + 4, low:high] = rows.reshape(SHARE, 4, width)
        done = slice(low, high)
        copy = pltpu.make_async_copy(ready.at[:, :, done], out.at[:, :, done], sent.at[tile])
        copy.start()
        copies.append(copy)
    for copy in copies:
        copy.wait()


def multiply(pieces, block):
    place = lax.axis_index("x").astype(jnp.int32).reshape(1)
    return pl.pallas_call(
        product_kernel,
        out_shape=jax.ShapeDtypeStruct((SHARE, 16, ROWS), jnp.float32),
        in_specs=[pl.BlockSpec(memory_space=pltpu.SMEM)] + [VMEM] * 9,
        out_specs=pl.BlockSpec(memory_space=pl.ANY),
        scratch_shapes=[
            pltpu.VMEM((2, 4 * SLOT, HALF), jnp.bfloat16),
            pltpu.VMEM((4, FOUR, 384), jnp.float32),
            pltpu.VMEM((SHARE, 16, ROWS), jnp.float32),
            pltpu.SemaphoreType.DMA((4,)),
        ],
        compiler_params=pltpu.CompilerParams(vmem_limit_bytes=28 * 1024 * 1024),
        cost_estimate=pl.CostEstimate(
            flops=8 * FOUR * ROWS * TIME, bytes_accessed=2_400_000, transcendentals=0
        ),
    )(place, *pieces, block)


def on_device(series):
    window, wide = standardize_pieces(lax.all_to_all(pack(series), BULK, 0, 0, tiled=True))
    own = lax.dynamic_slice_in_dim(window, lax.rem(lax.axis_index(BULK), 8), SHARE, 0)
    gathered = lax.all_gather(lax.all_gather(wide, "zh"), ("y", "core"))

    part = lax.all_gather(own.reshape(SHARE, TIME // 128, 128), "zl")
    part = part.transpose(1, 0, 2, 3).reshape(FOUR, TIME)
    first, second = part[:, :HALF], part[:, HALF:]
    after_first, before_second = shift(first, "x", 1), shift(second, "x", -1)
    after_second, before_first = shift(second, "x", 1), shift(first, "x", -1)
    far_first, far_second = shift(after_first, "x", 1), shift(before_second, "x", -1)

    pieces = (first, before_first, far_first, after_first)
    pieces += (second, before_second, far_second, after_second)
    return multiply(pieces, order(gathered)).transpose(1, 0, 2)


def solution(mesh):
    split = Mesh(mesh.devices.reshape(SIZES), AXES)
    return jax.shard_map(
        on_device,
        mesh=split,
        in_specs=(P(("x", "zl"), BULK),),
        out_specs=P(None, BULK, ("x", "zl")),
        check_vma=False,
    )
```

```python
import jax
import jax.numpy as jnp
from jax import lax
from jax.experimental import pallas as pl
from jax.experimental.pallas import tpu as pltpu
from jax.sharding import Mesh, PartitionSpec as P

TIME = 3072
HALF = TIME // 2
AXES = ("x", "zl", "zh", "y", "core")
SIZES = (4, 4, 2, 8, 2)
BULK = ("zh", "y", "core")
SHARE = 33
FOUR = 4 * SHARE
SLOT = 144
WINDOW = 40
WIDE = TIME + 128
ROWS = 1056
GROUP = 8 * SHARE
EDGES = (0, 256, 512, 768, ROWS)

VMEM = pl.BlockSpec(memory_space=pltpu.VMEM)

epsilon = 1e-06


def standardize(rows, axes):
    average = jnp.sum(rows, axis=axes, keepdims=True) / TIME
    centered = rows - average
    variance = jnp.sum(centered * centered, axis=axes, keepdims=True) / TIME
    return (centered * lax.rsqrt(variance + epsilon)).astype(jnp.bfloat16)


def standardize_kernel(pieces, window, wide, rows, single):
    for source in range(32):
        start = 96 * source
        rows[:32, start : start + 96] = pieces[source, :, :96]
        for p in range(3):
            cut = slice(start + 32 * p, start + 32 * p + 32)
            rows[32:, cut] = pieces[source, 8 * p : 8 * p + 8, 96:]
            single[source : source + 1, 32 * p : 32 * p + 32] = pieces[
                source, 24 + p : 25 + p, 96:
            ]
    scores = standardize(rows[...], (1,))
    window[...] = scores
    wide[:, :TIME] = scores[:32]
    wide[:, TIME:] = jnp.zeros((32, 128), jnp.bfloat16)
    wide[:, TIME : TIME + 96] = standardize(single[:, :96], (0, 1))


def standardize_pieces(pieces):
    return pl.pallas_call(
        standardize_kernel,
        out_shape=(
            jax.ShapeDtypeStruct((WINDOW, TIME), jnp.bfloat16),
            jax.ShapeDtypeStruct((32, WIDE), jnp.bfloat16),
        ),
        in_specs=[VMEM],
        out_specs=(VMEM, VMEM),
        scratch_shapes=[
            pltpu.VMEM((WINDOW, TIME), jnp.float32),
            pltpu.VMEM((32, 128), jnp.float32),
        ],
        compiler_params=pltpu.CompilerParams(vmem_limit_bytes=8 * 1024 * 1024),
    )(pieces)


def pack_kernel(steps, packed, rows):
    rows[...] = steps[...].T
    for device in range(32):
        group, i = divmod(device, 8)
        start, single = GROUP * group + 32 * i, GROUP * group + 256 + i
        packed[device, :, :96] = rows[start : start + 32, :]
        for p in range(3):
            cut = slice(32 * p, 32 * p + 32)
            packed[device, 8 * p : 8 * p + 8, 96:] = rows[start + 32 : start + 40, cut]
            packed[device, 24 + p : 25 + p, 96:] = rows[single : single + 1, cut]
        packed[device, 27:, 96:] = jnp.zeros((5, 32), jnp.float32)


def pack(series):
    return pl.pallas_call(
        pack_kernel,
        out_shape=jax.ShapeDtypeStruct((32, 32, 128), jnp.float32),
        in_specs=[VMEM],
        out_specs=VMEM,
        scratch_shapes=[pltpu.VMEM((ROWS, 96), jnp.float32)],
        compiler_params=pltpu.CompilerParams(vmem_limit_bytes=8 * 1024 * 1024),
    )(series.T)


def shift(array, axis, by):
    size = lax.axis_size(axis)
    return lax.ppermute(array, axis, [(i, (i + by) % size) for i in range(size)])


def contract(first, second, block, low, high):
    product = 0.0
    for t, part in enumerate((first, second)):
        product += lax.dot_general(
            part[...],
            block[low:high, HALF * t : HALF * t + HALF],
            (((1,), (1,)), ((), ())),
            preferred_element_type=jnp.float32,
        )
    return product * (1.0 / TIME)


def near_kernel(*refs):
    pieces, refs = refs[:6], refs[6:]
    windows, block, near, held, raw, parts, singles, tail, direct, arrived = refs
    copies = {}
    for group in range(4):
        half, parity = divmod(group, 2)
        devices, steps = pl.ds(8 * parity, 8), pl.ds(0, TIME)
        if parity:
            copies[group] = [
                pltpu.make_async_copy(
                    windows.at[devices, half, :, steps], held.at[half], arrived.at[group]
                )
            ]
        else:
            copies[group] = [
                pltpu.make_async_copy(
                    windows.at[i, half, :, steps],
                    block.at[pl.ds(GROUP * group + 32 * i, 32), :],
                    direct.at[half, i],
                )
                for i in range(8)
            ]
        copies[group].append(
            pltpu.make_async_copy(
                windows.at[devices, half, :, pl.ds(TIME, 128)],
                raw.at[group],
                arrived.at[4 + group],
            )
        )
        for copy in copies[group]:
            copy.start()
    for t in range(2):
        for k in range(3):
            parts[t, SLOT * k : SLOT * k + FOUR, :] = pieces[3 * t + k][...]

    def multiply_rows(low, high):
        product = contract(parts.at[0], parts.at[1], block, low, high)
        for k in range(3):
            near[k, :, low:high] = product[SLOT * k : SLOT * k + FOUR, :]

    for copy in copies[0]:
        copy.wait()
    multiply_rows(EDGES[0], EDGES[1])
    for group in range(1, 4):
        for copy in copies[group]:
            copy.wait()
    for group in range(4):
        half, parity = divmod(group, 2)
        for i in range(8):
            start = GROUP * group + 32 * i
            if parity:
                block[start : start + 32, :] = held[half, i]
            singles[32 * i : 32 * i + 32, :] = raw[group, i].astype(jnp.float32)
        for source in range(32):
            steps = singles[pl.ds(source, 8, stride=32), :]
            tail[:, 96 * source : 96 * source + 96] = steps[:, :96]
        start = GROUP * group + 256
        block[start : start + 8, :] = tail[...].astype(jnp.bfloat16)
    for low, high in zip(EDGES[1:-1], EDGES[2:]):
        multiply_rows(low, high)


def far_kernel(place, first, second, block, near, out, turned, ready, sent):
    copies = []
    for tile, (low, high) in enumerate(zip(EDGES[:-1], EDGES[1:])):
        width = high - low
        product = contract(first, second, block, low, high)
        turned[2, :, :width] = product
        for n, k in enumerate((0, 1, 3)):
            turned[k, :, :width] = near[n, :, low:high]
        for x in range(4):
            rows = turned[lax.rem(x - place[0] + 4, 4), :, :width]
            ready[:, 4 * x : 4 * x + 4, low:high] = rows.reshape(SHARE, 4, width)
        done = slice(low, high)
        copy = pltpu.make_async_copy(ready.at[:, :, done], out.at[:, :, done], sent.at[tile])
        copy.start()
        copies.append(copy)
    for copy in copies:
        copy.wait()


def multiply_near(pieces, windows):
    return pl.pallas_call(
        near_kernel,
        out_shape=(
            jax.ShapeDtypeStruct((ROWS, TIME), jnp.bfloat16),
            jax.ShapeDtypeStruct((3, FOUR, ROWS), jnp.float32),
        ),
        in_specs=[VMEM] * 6 + [pl.BlockSpec(memory_space=pl.ANY)],
        out_specs=(VMEM, VMEM),
        scratch_shapes=[
            pltpu.VMEM((2, 8, 32, TIME), jnp.bfloat16),
            pltpu.VMEM((4, 8, 32, 128), jnp.bfloat16),
            pltpu.VMEM((2, 3 * SLOT, HALF), jnp.bfloat16),
            pltpu.VMEM((256, 128), jnp.float32),
            pltpu.VMEM((8, TIME), jnp.float32),
            pltpu.SemaphoreType.DMA((2, 8)),
            pltpu.SemaphoreType.DMA((8,)),
        ],
        compiler_params=pltpu.CompilerParams(vmem_limit_bytes=40 * 1024 * 1024),
        cost_estimate=pl.CostEstimate(
            flops=6 * FOUR * ROWS * TIME, bytes_accessed=14_000_000, transcendentals=0
        ),
    )(*pieces, windows)


def multiply_far(first, second, block, near):
    place = lax.axis_index("x").astype(jnp.int32).reshape(1)
    return pl.pallas_call(
        far_kernel,
        out_shape=jax.ShapeDtypeStruct((SHARE, 16, ROWS), jnp.float32),
        in_specs=[pl.BlockSpec(memory_space=pltpu.SMEM), VMEM, VMEM, VMEM, VMEM],
        out_specs=pl.BlockSpec(memory_space=pl.ANY),
        scratch_shapes=[
            pltpu.VMEM((4, FOUR, 384), jnp.float32),
            pltpu.VMEM((SHARE, 16, ROWS), jnp.float32),
            pltpu.SemaphoreType.DMA((4,)),
        ],
        compiler_params=pltpu.CompilerParams(vmem_limit_bytes=24 * 1024 * 1024),
        cost_estimate=pl.CostEstimate(
            flops=2 * FOUR * ROWS * TIME, bytes_accessed=8_000_000, transcendentals=0
        ),
    )(place, first, second, block, near)


def on_device(series):
    window, wide = standardize_pieces(lax.all_to_all(pack(series), BULK, 0, 0, tiled=True))
    own = lax.dynamic_slice_in_dim(window, lax.rem(lax.axis_index(BULK), 8), SHARE, 0)
    gathered = lax.all_gather(lax.all_gather(wide, "zh"), ("y", "core"))

    part = lax.all_gather(own.reshape(SHARE, TIME // 128, 128), "zl")
    part = part.transpose(1, 0, 2, 3).reshape(FOUR, TIME)
    first, second = part[:, :HALF], part[:, HALF:]
    after_first, before_second = shift(first, "x", 1), shift(second, "x", -1)
    after_second, before_first = shift(second, "x", 1), shift(first, "x", -1)
    far_first, far_second = shift(after_first, "x", 1), shift(before_second, "x", -1)

    pieces = (first, before_first, after_first, second, before_second, after_second)
    block, near = multiply_near(pieces, gathered)
    return multiply_far(far_first, far_second, block, near).transpose(1, 0, 2)


def solution(mesh):
    split = Mesh(mesh.devices.reshape(SIZES), AXES)
    return jax.shard_map(
        on_device,
        mesh=split,
        in_specs=(P(("x", "zl"), BULK),),
        out_specs=P(None, BULK, ("x", "zl")),
        check_vma=False,
    )
```

```python
import jax
import jax.numpy as jnp
from jax import lax
from jax.experimental import pallas as pl
from jax.experimental.pallas import tpu as pltpu
from jax.sharding import Mesh, PartitionSpec as P

TIME = 3072
HALF = TIME // 2
AXES = ("x", "zl", "zh", "y", "core")
SIZES = (4, 4, 2, 8, 2)
BULK = ("zh", "y", "core")
SHARE = 33
FOUR = 4 * SHARE
SLOT = 144
WINDOW = 40
WIDE = TIME + 128
ROWS = 1056
GROUP = 8 * SHARE
EDGES = (0, 256, 512, 768, ROWS)

VMEM = pl.BlockSpec(memory_space=pltpu.VMEM)

epsilon = 1e-06


def standardize(rows, axes):
    average = jnp.sum(rows, axis=axes, keepdims=True) / TIME
    centered = rows - average
    variance = jnp.sum(centered * centered, axis=axes, keepdims=True) / TIME
    return (centered * lax.rsqrt(variance + epsilon)).astype(jnp.bfloat16)


def standardize_kernel(pieces, window, wide, rows, single):
    for source in range(32):
        start = 96 * source
        rows[:32, start : start + 96] = pieces[source, :, :96]
        for p in range(3):
            cut = slice(start + 32 * p, start + 32 * p + 32)
            rows[32:, cut] = pieces[source, 8 * p : 8 * p + 8, 96:]
            single[source : source + 1, 32 * p : 32 * p + 32] = pieces[
                source, 24 + p : 25 + p, 96:
            ]
    scores = standardize(rows[...], (1,))
    window[...] = scores
    wide[:, :TIME] = scores[:32]
    wide[:, TIME:] = jnp.zeros((32, 128), jnp.bfloat16)
    wide[:, TIME : TIME + 96] = standardize(single[:, :96], (0, 1))


def standardize_pieces(pieces):
    return pl.pallas_call(
        standardize_kernel,
        out_shape=(
            jax.ShapeDtypeStruct((WINDOW, TIME), jnp.bfloat16),
            jax.ShapeDtypeStruct((32, WIDE), jnp.bfloat16),
        ),
        in_specs=[VMEM],
        out_specs=(VMEM, VMEM),
        scratch_shapes=[
            pltpu.VMEM((WINDOW, TIME), jnp.float32),
            pltpu.VMEM((32, 128), jnp.float32),
        ],
        compiler_params=pltpu.CompilerParams(vmem_limit_bytes=8 * 1024 * 1024),
    )(pieces)


def pack_kernel(steps, packed, rows):
    rows[...] = steps[...].T
    for device in range(32):
        group, i = divmod(device, 8)
        start, single = GROUP * group + 32 * i, GROUP * group + 256 + i
        packed[device, :, :96] = rows[start : start + 32, :]
        for p in range(3):
            cut = slice(32 * p, 32 * p + 32)
            packed[device, 8 * p : 8 * p + 8, 96:] = rows[start + 32 : start + 40, cut]
            packed[device, 24 + p : 25 + p, 96:] = rows[single : single + 1, cut]
        packed[device, 27:, 96:] = jnp.zeros((5, 32), jnp.float32)


def pack(series):
    return pl.pallas_call(
        pack_kernel,
        out_shape=jax.ShapeDtypeStruct((32, 32, 128), jnp.float32),
        in_specs=[VMEM],
        out_specs=VMEM,
        scratch_shapes=[pltpu.VMEM((ROWS, 96), jnp.float32)],
        compiler_params=pltpu.CompilerParams(vmem_limit_bytes=8 * 1024 * 1024),
    )(series.T)


def shift(array, axis, by):
    size = lax.axis_size(axis)
    return lax.ppermute(array, axis, [(i, (i + by) % size) for i in range(size)])


def contract(first, second, block, low, high):
    product = 0.0
    for t, part in enumerate((first, second)):
        product += lax.dot_general(
            part[...],
            block[low:high, HALF * t : HALF * t + HALF],
            (((1,), (1,)), ((), ())),
            preferred_element_type=jnp.float32,
        )
    return product * (1.0 / TIME)


def order_kernel(windows, block, held, singles, tail, arrived):
    copies = []
    for group in range(4):
        half, parity = divmod(group, 2)
        copy = pltpu.make_async_copy(
            windows.at[pl.ds(8 * parity, 8), half], held.at[group], arrived.at[group]
        )
        copy.start()
        copies.append(copy)
    for group in range(4):
        copies[group].wait()
        for i in range(8):
            start = GROUP * group + 32 * i
            block[start : start + 32, :] = held[group, i, :, :TIME]
            singles[32 * i : 32 * i + 32, :] = held[group, i, :, TIME:].astype(jnp.float32)
        for source in range(32):
            steps = singles[pl.ds(source, 8, stride=32), :]
            tail[:, 96 * source : 96 * source + 96] = steps[:, :96]
        start = GROUP * group + 256
        block[start : start + 8, :] = tail[...].astype(jnp.bfloat16)


def order(windows):
    return pl.pallas_call(
        order_kernel,
        out_shape=jax.ShapeDtypeStruct((ROWS, TIME), jnp.bfloat16),
        in_specs=[pl.BlockSpec(memory_space=pl.ANY)],
        out_specs=VMEM,
        scratch_shapes=[
            pltpu.VMEM((4, 8, 32, WIDE), jnp.bfloat16),
            pltpu.VMEM((256, 128), jnp.float32),
            pltpu.VMEM((8, TIME), jnp.float32),
            pltpu.SemaphoreType.DMA((4,)),
        ],
        compiler_params=pltpu.CompilerParams(vmem_limit_bytes=44 * 1024 * 1024),
        cost_estimate=pl.CostEstimate(flops=0, bytes_accessed=7_000_000, transcendentals=0),
    )(windows)


def near_kernel(place, *refs):
    pieces, (block, near, parts) = refs[:6], refs[6:]

    @pl.when(place[1] == 0)
    def _():
        for t in range(2):
            for k in range(3):
                parts[t, SLOT * k : SLOT * k + FOUR, :] = pieces[3 * t + k][...]
        for low, high in zip(EDGES[:-1], EDGES[1:]):
            product = contract(parts.at[0], parts.at[1], block, low, high)
            for k in range(3):
                near[k, :, low:high] = product[SLOT * k : SLOT * k + FOUR, :]


def final_kernel(place, *refs):
    pieces, refs = refs[:8], refs[8:]
    block, near, out, parts, turned, ready, sent = refs

    def write(multiply_tile):
        copies = []
        for tile, (low, high) in enumerate(zip(EDGES[:-1], EDGES[1:])):
            width = high - low
            multiply_tile(low, high)
            for x in range(4):
                rows = turned[lax.rem(x - place[0] + 4, 4), :, :width]
                ready[:, 4 * x : 4 * x + 4, low:high] = rows.reshape(SHARE, 4, width)
            done = slice(low, high)
            copy = pltpu.make_async_copy(
                ready.at[:, :, done], out.at[:, :, done], sent.at[tile]
            )
            copy.start()
            copies.append(copy)
        for copy in copies:
            copy.wait()

    def far_tile(low, high):
        turned[2, :, : high - low] = contract(pieces[2], pieces[6], block, low, high)
        for n, k in enumerate((0, 1, 3)):
            turned[k, :, : high - low] = near[n, :, low:high]

    def whole_tile(low, high):
        product = contract(parts.at[0], parts.at[1], block, low, high)
        for k in range(4):
            turned[k, :, : high - low] = product[SLOT * k : SLOT * k + FOUR, :]

    @pl.when(place[1] == 0)
    def _():
        write(far_tile)

    @pl.when(place[1] != 0)
    def _():
        for t in range(2):
            for k in range(4):
                parts[t, SLOT * k : SLOT * k + FOUR, :] = pieces[4 * t + k][...]
        write(whole_tile)


SMEM = pl.BlockSpec(memory_space=pltpu.SMEM)


def multiply_near(place, pieces, block):
    return pl.pallas_call(
        near_kernel,
        out_shape=jax.ShapeDtypeStruct((3, FOUR, ROWS), jnp.float32),
        in_specs=[SMEM] + [VMEM] * 7,
        out_specs=VMEM,
        scratch_shapes=[pltpu.VMEM((2, 3 * SLOT, HALF), jnp.bfloat16)],
        compiler_params=pltpu.CompilerParams(vmem_limit_bytes=24 * 1024 * 1024),
        cost_estimate=pl.CostEstimate(
            flops=6 * FOUR * ROWS * TIME, bytes_accessed=2_000_000, transcendentals=0
        ),
    )(place, *pieces, block)


def multiply(place, pieces, block, near):
    return pl.pallas_call(
        final_kernel,
        out_shape=jax.ShapeDtypeStruct((SHARE, 16, ROWS), jnp.float32),
        in_specs=[SMEM] + [VMEM] * 10,
        out_specs=pl.BlockSpec(memory_space=pl.ANY),
        scratch_shapes=[
            pltpu.VMEM((2, 4 * SLOT, HALF), jnp.bfloat16),
            pltpu.VMEM((4, FOUR, 384), jnp.float32),
            pltpu.VMEM((SHARE, 16, ROWS), jnp.float32),
            pltpu.SemaphoreType.DMA((4,)),
        ],
        compiler_params=pltpu.CompilerParams(vmem_limit_bytes=28 * 1024 * 1024),
        cost_estimate=pl.CostEstimate(
            flops=2 * FOUR * ROWS * TIME, bytes_accessed=2_400_000, transcendentals=0
        ),
    )(place, *pieces, block, near)


def on_device(series):
    window, wide = standardize_pieces(lax.all_to_all(pack(series), BULK, 0, 0, tiled=True))
    own = lax.dynamic_slice_in_dim(window, lax.rem(lax.axis_index(BULK), 8), SHARE, 0)
    gathered = lax.all_gather(lax.all_gather(wide, "zh"), ("y", "core"))

    part = lax.all_gather(own.reshape(SHARE, TIME // 128, 128), "zl")
    part = part.transpose(1, 0, 2, 3).reshape(FOUR, TIME)
    first, second = part[:, :HALF], part[:, HALF:]
    after_first, before_second = shift(first, "x", 1), shift(second, "x", -1)
    after_second, before_first = shift(second, "x", 1), shift(first, "x", -1)
    far_first, far_second = shift(after_first, "x", 1), shift(before_second, "x", -1)

    place = jnp.stack([lax.axis_index("x"), lax.axis_index("core")]).astype(jnp.int32)
    block = order(gathered)
    pieces = (first, before_first, after_first, second, before_second, after_second)
    near = multiply_near(place, pieces, block)
    pieces = (first, before_first, far_first, after_first)
    pieces += (second, before_second, far_second, after_second)
    return multiply(place, pieces, block, near).transpose(1, 0, 2)


def solution(mesh):
    split = Mesh(mesh.devices.reshape(SIZES), AXES)
    return jax.shard_map(
        on_device,
        mesh=split,
        in_specs=(P(("x", "zl"), BULK),),
        out_specs=P(None, BULK, ("x", "zl")),
        check_vma=False,
    )
```

```python
import jax
import jax.numpy as jnp
from jax import lax
from jax.experimental import pallas as pl
from jax.experimental.pallas import tpu as pltpu
from jax.sharding import Mesh, PartitionSpec as P

TIME = 3072
HALF = TIME // 2
AXES = ("x", "zl", "zh", "y", "core")
SIZES = (4, 4, 2, 8, 2)
BULK = ("zh", "y", "core")
SHARE = 33
FOUR = 4 * SHARE
SLOT = 144
WINDOW = 40
WIDE = TIME + 128
ROWS = 1056
GROUP = 8 * SHARE
EDGES = (0, 256, 512, 768, ROWS)

VMEM = pl.BlockSpec(memory_space=pltpu.VMEM)

epsilon = 1e-06


def standardize(rows, axes):
    average = jnp.sum(rows, axis=axes, keepdims=True) / TIME
    centered = rows - average
    variance = jnp.sum(centered * centered, axis=axes, keepdims=True) / TIME
    return (centered * lax.rsqrt(variance + epsilon)).astype(jnp.bfloat16)


def standardize_kernel(pieces, window, wide, rows, single):
    for source in range(32):
        start = 96 * source
        rows[:32, start : start + 96] = pieces[source, :, :96]
        for p in range(3):
            cut = slice(start + 32 * p, start + 32 * p + 32)
            rows[32:, cut] = pieces[source, 8 * p : 8 * p + 8, 96:]
            single[source : source + 1, 32 * p : 32 * p + 32] = pieces[
                source, 24 + p : 25 + p, 96:
            ]
    scores = standardize(rows[...], (1,))
    window[...] = scores
    wide[:, :TIME] = scores[:32]
    wide[:, TIME:] = jnp.zeros((32, 128), jnp.bfloat16)
    wide[:, TIME : TIME + 96] = standardize(single[:, :96], (0, 1))


def standardize_pieces(pieces):
    return pl.pallas_call(
        standardize_kernel,
        out_shape=(
            jax.ShapeDtypeStruct((WINDOW, TIME), jnp.bfloat16),
            jax.ShapeDtypeStruct((32, WIDE), jnp.bfloat16),
        ),
        in_specs=[VMEM],
        out_specs=(VMEM, VMEM),
        scratch_shapes=[
            pltpu.VMEM((WINDOW, TIME), jnp.float32),
            pltpu.VMEM((32, 128), jnp.float32),
        ],
        compiler_params=pltpu.CompilerParams(vmem_limit_bytes=8 * 1024 * 1024),
    )(pieces)


def pack_kernel(steps, packed, rows):
    rows[...] = steps[...].T
    for device in range(32):
        group, i = divmod(device, 8)
        start, single = GROUP * group + 32 * i, GROUP * group + 256 + i
        packed[device, :, :96] = rows[start : start + 32, :]
        for p in range(3):
            cut = slice(32 * p, 32 * p + 32)
            packed[device, 8 * p : 8 * p + 8, 96:] = rows[start + 32 : start + 40, cut]
            packed[device, 24 + p : 25 + p, 96:] = rows[single : single + 1, cut]
        packed[device, 27:, 96:] = jnp.zeros((5, 32), jnp.float32)


def pack(series):
    return pl.pallas_call(
        pack_kernel,
        out_shape=jax.ShapeDtypeStruct((32, 32, 128), jnp.float32),
        in_specs=[VMEM],
        out_specs=VMEM,
        scratch_shapes=[pltpu.VMEM((ROWS, 96), jnp.float32)],
        compiler_params=pltpu.CompilerParams(vmem_limit_bytes=8 * 1024 * 1024),
    )(series.T)


def shift(array, axis, by):
    size = lax.axis_size(axis)
    return lax.ppermute(array, axis, [(i, (i + by) % size) for i in range(size)])


def contract(first, second, block, low, high):
    product = 0.0
    for t, part in enumerate((first, second)):
        product += lax.dot_general(
            part[...],
            block[low:high, HALF * t : HALF * t + HALF],
            (((1,), (1,)), ((), ())),
            preferred_element_type=jnp.float32,
        )
    return product * (1.0 / TIME)


def near_kernel(*refs):
    pieces, refs = refs[:6], refs[6:]
    windows, block, near, held, raw, parts, singles, tail, direct, arrived = refs
    copies = {}
    for group in range(4):
        half, parity = divmod(group, 2)
        devices, steps = pl.ds(8 * parity, 8), pl.ds(0, TIME)
        if parity:
            copies[group] = [
                pltpu.make_async_copy(
                    windows.at[devices, half, :, steps], held.at[half], arrived.at[group]
                )
            ]
        else:
            copies[group] = [
                pltpu.make_async_copy(
                    windows.at[i, half, :, steps],
                    block.at[pl.ds(GROUP * group + 32 * i, 32), :],
                    direct.at[half, i],
                )
                for i in range(8)
            ]
        copies[group].append(
            pltpu.make_async_copy(
                windows.at[devices, half, :, pl.ds(TIME, 128)],
                raw.at[group],
                arrived.at[4 + group],
            )
        )
        for copy in copies[group]:
            copy.start()
    for t in range(2):
        for k in range(3):
            parts[t, SLOT * k : SLOT * k + FOUR, :] = pieces[3 * t + k][...]

    def multiply_rows(low, high):
        product = contract(parts.at[0], parts.at[1], block, low, high)
        for k in range(3):
            near[k, :, low:high] = product[SLOT * k : SLOT * k + FOUR, :]

    for group in range(4):
        for copy in copies[group]:
            copy.wait()
    for group in range(4):
        half, parity = divmod(group, 2)
        for i in range(8):
            start = GROUP * group + 32 * i
            if parity:
                block[start : start + 32, :] = held[half, i]
            singles[32 * i : 32 * i + 32, :] = raw[group, i].astype(jnp.float32)
        for source in range(32):
            steps = singles[pl.ds(source, 8, stride=32), :]
            tail[:, 96 * source : 96 * source + 96] = steps[:, :96]
        start = GROUP * group + 256
        block[start : start + 8, :] = tail[...].astype(jnp.bfloat16)
    for low, high in zip(EDGES[:-1], EDGES[1:]):
        multiply_rows(low, high)


def far_kernel(place, first, second, block, near, out, turned, ready, sent):
    copies = []
    for tile, (low, high) in enumerate(zip(EDGES[:-1], EDGES[1:])):
        width = high - low
        product = contract(first, second, block, low, high)
        turned[2, :, :width] = product
        for n, k in enumerate((0, 1, 3)):
            turned[k, :, :width] = near[n, :, low:high]
        for x in range(4):
            rows = turned[lax.rem(x - place[0] + 4, 4), :, :width]
            ready[:, 4 * x : 4 * x + 4, low:high] = rows.reshape(SHARE, 4, width)
        done = slice(low, high)
        copy = pltpu.make_async_copy(ready.at[:, :, done], out.at[:, :, done], sent.at[tile])
        copy.start()
        copies.append(copy)
    for copy in copies:
        copy.wait()


def multiply_near(pieces, windows):
    return pl.pallas_call(
        near_kernel,
        out_shape=(
            jax.ShapeDtypeStruct((ROWS, TIME), jnp.bfloat16),
            jax.ShapeDtypeStruct((3, FOUR, ROWS), jnp.float32),
        ),
        in_specs=[VMEM] * 6 + [pl.BlockSpec(memory_space=pl.ANY)],
        out_specs=(VMEM, VMEM),
        scratch_shapes=[
            pltpu.VMEM((2, 8, 32, TIME), jnp.bfloat16),
            pltpu.VMEM((4, 8, 32, 128), jnp.bfloat16),
            pltpu.VMEM((2, 3 * SLOT, HALF), jnp.bfloat16),
            pltpu.VMEM((256, 128), jnp.float32),
            pltpu.VMEM((8, TIME), jnp.float32),
            pltpu.SemaphoreType.DMA((2, 8)),
            pltpu.SemaphoreType.DMA((8,)),
        ],
        compiler_params=pltpu.CompilerParams(vmem_limit_bytes=40 * 1024 * 1024),
        cost_estimate=pl.CostEstimate(
            flops=6 * FOUR * ROWS * TIME, bytes_accessed=14_000_000, transcendentals=0
        ),
    )(*pieces, windows)


def multiply_far(first, second, block, near):
    place = lax.axis_index("x").astype(jnp.int32).reshape(1)
    return pl.pallas_call(
        far_kernel,
        out_shape=jax.ShapeDtypeStruct((SHARE, 16, ROWS), jnp.float32),
        in_specs=[pl.BlockSpec(memory_space=pltpu.SMEM), VMEM, VMEM, VMEM, VMEM],
        out_specs=pl.BlockSpec(memory_space=pl.ANY),
        scratch_shapes=[
            pltpu.VMEM((4, FOUR, 384), jnp.float32),
            pltpu.VMEM((SHARE, 16, ROWS), jnp.float32),
            pltpu.SemaphoreType.DMA((4,)),
        ],
        compiler_params=pltpu.CompilerParams(vmem_limit_bytes=24 * 1024 * 1024),
        cost_estimate=pl.CostEstimate(
            flops=2 * FOUR * ROWS * TIME, bytes_accessed=8_000_000, transcendentals=0
        ),
    )(place, first, second, block, near)


def on_device(series):
    window, wide = standardize_pieces(lax.all_to_all(pack(series), BULK, 0, 0, tiled=True))
    own = lax.dynamic_slice_in_dim(window, lax.rem(lax.axis_index(BULK), 8), SHARE, 0)
    gathered = lax.all_gather(lax.all_gather(wide, "zh"), ("y", "core"))

    part = lax.all_gather(own.reshape(SHARE, TIME // 128, 128), "zl")
    part = part.transpose(1, 0, 2, 3).reshape(FOUR, TIME)
    first, second = part[:, :HALF], part[:, HALF:]
    after_first, before_second = shift(first, "x", 1), shift(second, "x", -1)
    after_second, before_first = shift(second, "x", 1), shift(first, "x", -1)
    far_first, far_second = shift(after_first, "x", 1), shift(before_second, "x", -1)

    pieces = (first, before_first, after_first, second, before_second, after_second)
    block, near = multiply_near(pieces, gathered)
    return multiply_far(far_first, far_second, block, near).transpose(1, 0, 2)


def solution(mesh):
    split = Mesh(mesh.devices.reshape(SIZES), AXES)
    return jax.shard_map(
        on_device,
        mesh=split,
        in_specs=(P(("x", "zl"), BULK),),
        out_specs=P(None, BULK, ("x", "zl")),
        check_vma=False,
    )
```

```python
import jax
import jax.numpy as jnp
from jax import lax
from jax.experimental import pallas as pl
from jax.experimental.pallas import tpu as pltpu
from jax.sharding import Mesh, PartitionSpec as P

TIME = 3072
HALF = TIME // 2
AXES = ("x", "zl", "zh", "y", "core")
SIZES = (4, 4, 2, 8, 2)
BULK = ("zh", "y", "core")
SHARE = 33
FOUR = 4 * SHARE
SLOT = 136
WINDOW = 40
WIDE = TIME + 128
ROWS = 1056
GROUP = 8 * SHARE
EDGES = (0, 256, 512, 768, ROWS)

VMEM = pl.BlockSpec(memory_space=pltpu.VMEM)

epsilon = 1e-06


def standardize(rows, axes):
    average = jnp.sum(rows, axis=axes, keepdims=True) / TIME
    centered = rows - average
    variance = jnp.sum(centered * centered, axis=axes, keepdims=True) / TIME
    return (centered * lax.rsqrt(variance + epsilon)).astype(jnp.bfloat16)


def standardize_kernel(pieces, window, wide, rows, single):
    for source in range(32):
        start = 96 * source
        rows[:32, start : start + 96] = pieces[source, :, :96]
        for p in range(3):
            cut = slice(start + 32 * p, start + 32 * p + 32)
            rows[32:, cut] = pieces[source, 8 * p : 8 * p + 8, 96:]
            single[source : source + 1, 32 * p : 32 * p + 32] = pieces[
                source, 24 + p : 25 + p, 96:
            ]
    scores = standardize(rows[...], (1,))
    window[...] = scores
    wide[:, :TIME] = scores[:32]
    wide[:, TIME:] = jnp.zeros((32, 128), jnp.bfloat16)
    wide[:, TIME : TIME + 96] = standardize(single[:, :96], (0, 1))


def standardize_pieces(pieces):
    return pl.pallas_call(
        standardize_kernel,
        out_shape=(
            jax.ShapeDtypeStruct((WINDOW, TIME), jnp.bfloat16),
            jax.ShapeDtypeStruct((32, WIDE), jnp.bfloat16),
        ),
        in_specs=[VMEM],
        out_specs=(VMEM, VMEM),
        scratch_shapes=[
            pltpu.VMEM((WINDOW, TIME), jnp.float32),
            pltpu.VMEM((32, 128), jnp.float32),
        ],
        compiler_params=pltpu.CompilerParams(vmem_limit_bytes=8 * 1024 * 1024),
    )(pieces)


def pack_kernel(steps, packed, rows):
    rows[...] = steps[...].T
    for device in range(32):
        group, i = divmod(device, 8)
        start, single = GROUP * group + 32 * i, GROUP * group + 256 + i
        packed[device, :, :96] = rows[start : start + 32, :]
        for p in range(3):
            cut = slice(32 * p, 32 * p + 32)
            packed[device, 8 * p : 8 * p + 8, 96:] = rows[start + 32 : start + 40, cut]
            packed[device, 24 + p : 25 + p, 96:] = rows[single : single + 1, cut]
        packed[device, 27:, 96:] = jnp.zeros((5, 32), jnp.float32)


def pack(series):
    return pl.pallas_call(
        pack_kernel,
        out_shape=jax.ShapeDtypeStruct((32, 32, 128), jnp.float32),
        in_specs=[VMEM],
        out_specs=VMEM,
        scratch_shapes=[pltpu.VMEM((ROWS, 96), jnp.float32)],
        compiler_params=pltpu.CompilerParams(vmem_limit_bytes=8 * 1024 * 1024),
    )(series.T)


def shift(array, axis, by):
    size = lax.axis_size(axis)
    return lax.ppermute(array, axis, [(i, (i + by) % size) for i in range(size)])


def contract(first, second, block, low, high):
    product = 0.0
    for t, part in enumerate((first, second)):
        product += lax.dot_general(
            part[...],
            block[low:high, HALF * t : HALF * t + HALF],
            (((1,), (1,)), ((), ())),
            preferred_element_type=jnp.float32,
        )
    return product * (1.0 / TIME)


def near_kernel(*refs):
    pieces, refs = refs[:6], refs[6:]
    windows, block, near, held, raw, parts, singles, tail, direct, arrived = refs
    copies = {}
    for group in range(4):
        half, parity = divmod(group, 2)
        devices, steps = pl.ds(8 * parity, 8), pl.ds(0, TIME)
        if parity:
            copies[group] = [
                pltpu.make_async_copy(
                    windows.at[devices, half, :, steps], held.at[half], arrived.at[group]
                )
            ]
        else:
            copies[group] = [
                pltpu.make_async_copy(
                    windows.at[i, half, :, steps],
                    block.at[pl.ds(GROUP * group + 32 * i, 32), :],
                    direct.at[half, i],
                )
                for i in range(8)
            ]
        copies[group].append(
            pltpu.make_async_copy(
                windows.at[devices, half, :, pl.ds(TIME, 128)],
                raw.at[group],
                arrived.at[4 + group],
            )
        )
        for copy in copies[group]:
            copy.start()
    for t in range(2):
        for k in range(3):
            parts[t, SLOT * k : SLOT * k + FOUR, :] = pieces[3 * t + k][...]

    def multiply_rows(low, high):
        product = contract(parts.at[0], parts.at[1], block, low, high)
        for k in range(3):
            near[k, :, low:high] = product[SLOT * k : SLOT * k + FOUR, :]

    for group in range(4):
        for copy in copies[group]:
            copy.wait()
    for group in range(4):
        half, parity = divmod(group, 2)
        for i in range(8):
            start = GROUP * group + 32 * i
            if parity:
                block[start : start + 32, :] = held[half, i]
            singles[32 * i : 32 * i + 32, :] = raw[group, i].astype(jnp.float32)
        for source in range(32):
            steps = singles[pl.ds(source, 8, stride=32), :]
            tail[:, 96 * source : 96 * source + 96] = steps[:, :96]
        start = GROUP * group + 256
        block[start : start + 8, :] = tail[...].astype(jnp.bfloat16)
    for low, high in zip(EDGES[:-1], EDGES[1:]):
        multiply_rows(low, high)


def far_kernel(place, first, second, block, near, out, turned, ready, sent):
    copies = []
    for tile, (low, high) in enumerate(zip(EDGES[:-1], EDGES[1:])):
        width = high - low
        product = contract(first, second, block, low, high)
        turned[2, :, :width] = product
        for n, k in enumerate((0, 1, 3)):
            turned[k, :, :width] = near[n, :, low:high]
        for x in range(4):
            rows = turned[lax.rem(x - place[0] + 4, 4), :, :width]
            ready[:, 4 * x : 4 * x + 4, low:high] = rows.reshape(SHARE, 4, width)
        done = slice(low, high)
        copy = pltpu.make_async_copy(ready.at[:, :, done], out.at[:, :, done], sent.at[tile])
        copy.start()
        copies.append(copy)
    for copy in copies:
        copy.wait()


def multiply_near(pieces, windows):
    return pl.pallas_call(
        near_kernel,
        out_shape=(
            jax.ShapeDtypeStruct((ROWS, TIME), jnp.bfloat16),
            jax.ShapeDtypeStruct((3, FOUR, ROWS), jnp.float32),
        ),
        in_specs=[VMEM] * 6 + [pl.BlockSpec(memory_space=pl.ANY)],
        out_specs=(VMEM, VMEM),
        scratch_shapes=[
            pltpu.VMEM((2, 8, 32, TIME), jnp.bfloat16),
            pltpu.VMEM((4, 8, 32, 128), jnp.bfloat16),
            pltpu.VMEM((2, 3 * SLOT, HALF), jnp.bfloat16),
            pltpu.VMEM((256, 128), jnp.float32),
            pltpu.VMEM((8, TIME), jnp.float32),
            pltpu.SemaphoreType.DMA((2, 8)),
            pltpu.SemaphoreType.DMA((8,)),
        ],
        compiler_params=pltpu.CompilerParams(vmem_limit_bytes=40 * 1024 * 1024),
        cost_estimate=pl.CostEstimate(
            flops=6 * FOUR * ROWS * TIME, bytes_accessed=14_000_000, transcendentals=0
        ),
    )(*pieces, windows)


def multiply_far(first, second, block, near):
    place = lax.axis_index("x").astype(jnp.int32).reshape(1)
    return pl.pallas_call(
        far_kernel,
        out_shape=jax.ShapeDtypeStruct((SHARE, 16, ROWS), jnp.float32),
        in_specs=[pl.BlockSpec(memory_space=pltpu.SMEM), VMEM, VMEM, VMEM, VMEM],
        out_specs=pl.BlockSpec(memory_space=pl.ANY),
        scratch_shapes=[
            pltpu.VMEM((4, FOUR, 384), jnp.float32),
            pltpu.VMEM((SHARE, 16, ROWS), jnp.float32),
            pltpu.SemaphoreType.DMA((4,)),
        ],
        compiler_params=pltpu.CompilerParams(vmem_limit_bytes=24 * 1024 * 1024),
        cost_estimate=pl.CostEstimate(
            flops=2 * FOUR * ROWS * TIME, bytes_accessed=8_000_000, transcendentals=0
        ),
    )(place, first, second, block, near)


def on_device(series):
    window, wide = standardize_pieces(lax.all_to_all(pack(series), BULK, 0, 0, tiled=True))
    own = lax.dynamic_slice_in_dim(window, lax.rem(lax.axis_index(BULK), 8), SHARE, 0)
    gathered = lax.all_gather(lax.all_gather(wide, "zh"), ("y", "core"))

    part = lax.all_gather(own.reshape(SHARE, TIME // 128, 128), "zl")
    part = part.transpose(1, 0, 2, 3).reshape(FOUR, TIME)
    first, second = part[:, :HALF], part[:, HALF:]
    after_first, before_second = shift(first, "x", 1), shift(second, "x", -1)
    after_second, before_first = shift(second, "x", 1), shift(first, "x", -1)
    far_first, far_second = shift(after_first, "x", 1), shift(before_second, "x", -1)

    pieces = (first, before_first, after_first, second, before_second, after_second)
    block, near = multiply_near(pieces, gathered)
    return multiply_far(far_first, far_second, block, near).transpose(1, 0, 2)


def solution(mesh):
    split = Mesh(mesh.devices.reshape(SIZES), AXES)
    return jax.shard_map(
        on_device,
        mesh=split,
        in_specs=(P(("x", "zl"), BULK),),
        out_specs=P(None, BULK, ("x", "zl")),
        check_vma=False,
    )
```

```python
import jax
import jax.numpy as jnp
from jax import lax
from jax.experimental import pallas as pl
from jax.experimental.pallas import tpu as pltpu
from jax.sharding import Mesh, PartitionSpec as P

TIME = 3072
HALF = TIME // 2
AXES = ("x", "zl", "zh", "y", "core")
SIZES = (4, 4, 2, 8, 2)
BULK = ("zh", "y", "core")
SHARE = 33
FOUR = 4 * SHARE
SLOT = 144
WINDOW = 40
WIDE = TIME + 128
ROWS = 1056
GROUP = 8 * SHARE
EDGES = (0, 512, ROWS)

VMEM = pl.BlockSpec(memory_space=pltpu.VMEM)

epsilon = 1e-06


def standardize(rows, axes):
    average = jnp.sum(rows, axis=axes, keepdims=True) / TIME
    centered = rows - average
    variance = jnp.sum(centered * centered, axis=axes, keepdims=True) / TIME
    return (centered * lax.rsqrt(variance + epsilon)).astype(jnp.bfloat16)


def standardize_kernel(pieces, window, wide, rows, single):
    for source in range(32):
        start = 96 * source
        rows[:32, start : start + 96] = pieces[source, :, :96]
        for p in range(3):
            cut = slice(start + 32 * p, start + 32 * p + 32)
            rows[32:, cut] = pieces[source, 8 * p : 8 * p + 8, 96:]
            single[source : source + 1, 32 * p : 32 * p + 32] = pieces[
                source, 24 + p : 25 + p, 96:
            ]
    scores = standardize(rows[...], (1,))
    window[...] = scores
    wide[:, :TIME] = scores[:32]
    wide[:, TIME:] = jnp.zeros((32, 128), jnp.bfloat16)
    wide[:, TIME : TIME + 96] = standardize(single[:, :96], (0, 1))


def standardize_pieces(pieces):
    return pl.pallas_call(
        standardize_kernel,
        out_shape=(
            jax.ShapeDtypeStruct((WINDOW, TIME), jnp.bfloat16),
            jax.ShapeDtypeStruct((32, WIDE), jnp.bfloat16),
        ),
        in_specs=[VMEM],
        out_specs=(VMEM, VMEM),
        scratch_shapes=[
            pltpu.VMEM((WINDOW, TIME), jnp.float32),
            pltpu.VMEM((32, 128), jnp.float32),
        ],
        compiler_params=pltpu.CompilerParams(vmem_limit_bytes=8 * 1024 * 1024),
    )(pieces)


def pack_kernel(steps, packed, rows):
    rows[...] = steps[...].T
    for device in range(32):
        group, i = divmod(device, 8)
        start, single = GROUP * group + 32 * i, GROUP * group + 256 + i
        packed[device, :, :96] = rows[start : start + 32, :]
        for p in range(3):
            cut = slice(32 * p, 32 * p + 32)
            packed[device, 8 * p : 8 * p + 8, 96:] = rows[start + 32 : start + 40, cut]
            packed[device, 24 + p : 25 + p, 96:] = rows[single : single + 1, cut]
        packed[device, 27:, 96:] = jnp.zeros((5, 32), jnp.float32)


def pack(series):
    return pl.pallas_call(
        pack_kernel,
        out_shape=jax.ShapeDtypeStruct((32, 32, 128), jnp.float32),
        in_specs=[VMEM],
        out_specs=VMEM,
        scratch_shapes=[pltpu.VMEM((ROWS, 96), jnp.float32)],
        compiler_params=pltpu.CompilerParams(vmem_limit_bytes=8 * 1024 * 1024),
    )(series.T)


def shift(array, axis, by):
    size = lax.axis_size(axis)
    return lax.ppermute(array, axis, [(i, (i + by) % size) for i in range(size)])


def contract(first, second, block, low, high):
    product = 0.0
    for t, part in enumerate((first, second)):
        product += lax.dot_general(
            part[...],
            block[low:high, HALF * t : HALF * t + HALF],
            (((1,), (1,)), ((), ())),
            preferred_element_type=jnp.float32,
        )
    return product * (1.0 / TIME)


def near_kernel(*refs):
    pieces, refs = refs[:6], refs[6:]
    windows, block, near, held, raw, parts, singles, tail, direct, arrived = refs
    copies = {}
    for group in range(4):
        half, parity = divmod(group, 2)
        devices, steps = pl.ds(8 * parity, 8), pl.ds(0, TIME)
        if parity:
            copies[group] = [
                pltpu.make_async_copy(
                    windows.at[devices, half, :, steps], held.at[half], arrived.at[group]
                )
            ]
        else:
            copies[group] = [
                pltpu.make_async_copy(
                    windows.at[i, half, :, steps],
                    block.at[pl.ds(GROUP * group + 32 * i, 32), :],
                    direct.at[half, i],
                )
                for i in range(8)
            ]
        copies[group].append(
            pltpu.make_async_copy(
                windows.at[devices, half, :, pl.ds(TIME, 128)],
                raw.at[group],
                arrived.at[4 + group],
            )
        )
        for copy in copies[group]:
            copy.start()
    for t in range(2):
        for k in range(3):
            parts[t, SLOT * k : SLOT * k + FOUR, :] = pieces[3 * t + k][...]

    def multiply_rows(low, high):
        product = contract(parts.at[0], parts.at[1], block, low, high)
        for k in range(3):
            near[k, :, low:high] = product[SLOT * k : SLOT * k + FOUR, :]

    for group in range(4):
        for copy in copies[group]:
            copy.wait()
    for group in range(4):
        half, parity = divmod(group, 2)
        for i in range(8):
            start = GROUP * group + 32 * i
            if parity:
                block[start : start + 32, :] = held[half, i]
            singles[32 * i : 32 * i + 32, :] = raw[group, i].astype(jnp.float32)
        for source in range(32):
            steps = singles[pl.ds(source, 8, stride=32), :]
            tail[:, 96 * source : 96 * source + 96] = steps[:, :96]
        start = GROUP * group + 256
        block[start : start + 8, :] = tail[...].astype(jnp.bfloat16)
    for low, high in zip(EDGES[:-1], EDGES[1:]):
        multiply_rows(low, high)


def far_kernel(place, first, second, block, near, out, turned, ready, sent):
    copies = []
    for tile, (low, high) in enumerate(zip(EDGES[:-1], EDGES[1:])):
        width = high - low
        product = contract(first, second, block, low, high)
        turned[2, :, :width] = product
        for n, k in enumerate((0, 1, 3)):
            turned[k, :, :width] = near[n, :, low:high]
        for x in range(4):
            rows = turned[lax.rem(x - place[0] + 4, 4), :, :width]
            ready[:, 4 * x : 4 * x + 4, low:high] = rows.reshape(SHARE, 4, width)
        done = slice(low, high)
        copy = pltpu.make_async_copy(ready.at[:, :, done], out.at[:, :, done], sent.at[tile])
        copy.start()
        copies.append(copy)
    for copy in copies:
        copy.wait()


def multiply_near(pieces, windows):
    return pl.pallas_call(
        near_kernel,
        out_shape=(
            jax.ShapeDtypeStruct((ROWS, TIME), jnp.bfloat16),
            jax.ShapeDtypeStruct((3, FOUR, ROWS), jnp.float32),
        ),
        in_specs=[VMEM] * 6 + [pl.BlockSpec(memory_space=pl.ANY)],
        out_specs=(VMEM, VMEM),
        scratch_shapes=[
            pltpu.VMEM((2, 8, 32, TIME), jnp.bfloat16),
            pltpu.VMEM((4, 8, 32, 128), jnp.bfloat16),
            pltpu.VMEM((2, 3 * SLOT, HALF), jnp.bfloat16),
            pltpu.VMEM((256, 128), jnp.float32),
            pltpu.VMEM((8, TIME), jnp.float32),
            pltpu.SemaphoreType.DMA((2, 8)),
            pltpu.SemaphoreType.DMA((8,)),
        ],
        compiler_params=pltpu.CompilerParams(vmem_limit_bytes=40 * 1024 * 1024),
        cost_estimate=pl.CostEstimate(
            flops=6 * FOUR * ROWS * TIME, bytes_accessed=14_000_000, transcendentals=0
        ),
    )(*pieces, windows)


def multiply_far(first, second, block, near):
    place = lax.axis_index("x").astype(jnp.int32).reshape(1)
    return pl.pallas_call(
        far_kernel,
        out_shape=jax.ShapeDtypeStruct((SHARE, 16, ROWS), jnp.float32),
        in_specs=[pl.BlockSpec(memory_space=pltpu.SMEM), VMEM, VMEM, VMEM, VMEM],
        out_specs=pl.BlockSpec(memory_space=pl.ANY),
        scratch_shapes=[
            pltpu.VMEM((4, FOUR, 640), jnp.float32),
            pltpu.VMEM((SHARE, 16, ROWS), jnp.float32),
            pltpu.SemaphoreType.DMA((4,)),
        ],
        compiler_params=pltpu.CompilerParams(vmem_limit_bytes=24 * 1024 * 1024),
        cost_estimate=pl.CostEstimate(
            flops=2 * FOUR * ROWS * TIME, bytes_accessed=8_000_000, transcendentals=0
        ),
    )(place, first, second, block, near)


def on_device(series):
    window, wide = standardize_pieces(lax.all_to_all(pack(series), BULK, 0, 0, tiled=True))
    own = lax.dynamic_slice_in_dim(window, lax.rem(lax.axis_index(BULK), 8), SHARE, 0)
    gathered = lax.all_gather(lax.all_gather(wide, "zh"), ("y", "core"))

    part = lax.all_gather(own.reshape(SHARE, TIME // 128, 128), "zl")
    part = part.transpose(1, 0, 2, 3).reshape(FOUR, TIME)
    first, second = part[:, :HALF], part[:, HALF:]
    after_first, before_second = shift(first, "x", 1), shift(second, "x", -1)
    after_second, before_first = shift(second, "x", 1), shift(first, "x", -1)
    far_first, far_second = shift(after_first, "x", 1), shift(before_second, "x", -1)

    pieces = (first, before_first, after_first, second, before_second, after_second)
    block, near = multiply_near(pieces, gathered)
    return multiply_far(far_first, far_second, block, near).transpose(1, 0, 2)


def solution(mesh):
    split = Mesh(mesh.devices.reshape(SIZES), AXES)
    return jax.shard_map(
        on_device,
        mesh=split,
        in_specs=(P(("x", "zl"), BULK),),
        out_specs=P(None, BULK, ("x", "zl")),
        check_vma=False,
    )
```
